512 devices in a mesh: ctx: 32 (over z, y_hi), tp: 16 (over y_lo, x, core).
Axes of the slice: x: 4, y: 4 (y_hi: 2, y_lo: 2; y = y_hi * 2 + y_lo), z: 16, core: 2. Of those that a mesh axis runs over, the one named last changes fastest.
Arguments:
- queries: bfloat16 [4096, 4096], P('ctx', 'tp'), may hold values from -10 to 10
- keys: bfloat16 [4096, 4096], P('ctx', 'tp'), may hold values from -10 to 10
- values: bfloat16 [4096, 4096], P('ctx', 'tp'), may hold values from -6 to 6
- attn_out: bfloat16 [4096, 4096], P('ctx', 'tp'), may hold values from -6 to 6
- out_grad: bfloat16 [4096, 6144], P('ctx', 'tp'), may hold values from -6 to 6
- out_weight: bfloat16 [4096, 6144], P('tp'), may hold values from -0.09375 to 0.09375
- token_sizes: int32 [4096], P('ctx'), may hold values from 1 to 16
Outputs:
- query_grad: bfloat16 [4096, 4096], P('ctx', 'tp')
- key_grad: bfloat16 [4096, 4096], P('ctx', 'tp')
- value_grad: bfloat16 [4096, 4096], P('ctx', 'tp')
The draws below stay inside these ranges and needn't reach their ends.
All inputs are finite; a program needn't handle non-finite values.
Results may differ from the reference program's by a relative error of at most 0.0085.
Values may be sent and summed in bfloat16 or wider, within the bound.
A program may use at most 64 MiB of HBM per device.

```python
import jax
import jax.numpy as jnp
from jax import lax

D = 6144
HEADS = 32
HD = 128
TOKENS = 4096


def draw_queries(key, part):
    key = jax.random.fold_in(key, 1)
    result = jnp.clip(jax.random.normal(key, (TOKENS, HEADS * HD), jnp.float32), -6.0, 6.0)
    return result.astype(jnp.bfloat16)


def draw_keys(key, part):
    key = jax.random.fold_in(key, 2)
    result = jnp.clip(jax.random.normal(key, (TOKENS, HEADS * HD), jnp.float32), -6.0, 6.0)
    return result.astype(jnp.bfloat16)


def place_ends(values, key, least, high):
    extent = values.shape
    index_at = [jax.random.randint(jax.random.fold_in(key, axis), (), 0, extent[axis]) for axis in range(len(extent))]
    values = values.at[tuple(index_at)].set(least)
    longest = extent.index(max(extent))
    index_at[longest] = (index_at[longest] + 1) % extent[longest]
    return values.at[tuple(index_at)].set(high)


def block_scale(key, shape, cuts, smallest, high):
    gain = 1.0
    for axis_at, shards_of in cuts:
        draws = jax.random.uniform(jax.random.fold_in(jax.random.fold_in(key, 6), axis_at), (shards_of,), jnp.float32, smallest / len(cuts), high / len(cuts))
        gain = gain * jnp.repeat(jnp.exp(draws), shape[axis_at] // shards_of).reshape((-1,) + (1,) * (len(shape) - 1 - axis_at))
    return gain


def centred(stream_key, dims, width, bound, shards=(), kind=jnp.bfloat16):
    values = width * jax.random.normal(stream_key, dims, jnp.float32)
    if shards:
        values = values * block_scale(stream_key, dims, shards, -0.22, 0.18)
    return jnp.clip(values, -bound, bound).astype(kind)


def setup_inputs(seed: int = 0) -> dict:
    splits = jax.random.split(jax.random.key(seed), 8)
    queries = draw_queries(jax.random.fold_in(splits[7], 71), 0)
    keys = draw_keys(jax.random.fold_in(splits[7], 71), 0)
    values = centred(splits[2], (TOKENS, HEADS * HD), 1.0, 6.0, ((0, 32), (1, 16)))
    attn_out = centred(splits[3], (TOKENS, HEADS * HD), 1.0, 6.0, ((0, 32), (1, 16)))
    out_grad = centred(splits[4], (TOKENS, D), 1.0, 6.0, ((0, 32), (1, 16)))
    out_weight = centred(splits[5], (HEADS * HD, D), (HEADS * HD) ** -0.5, 0.09375, ((0, 16),))
    token_sizes = place_ends(jax.random.randint(splits[6], (TOKENS,), 1, 17), jax.random.fold_in(splits[6], 1), 1, 16).astype(jnp.int32)
    return dict(queries=queries, keys=keys, values=values, attn_out=attn_out, out_grad=out_grad, out_weight=out_weight, token_sizes=token_sizes)


def head_backward(operands):
    query, key, value, grad, output, bias = operands
    scale = 1.0 / (HD ** 0.5)
    scores = scale * jnp.dot(query, key.T, preferred_element_type=jnp.float32) + bias[None, :]
    highest = jnp.max(scores, axis=-1)
    lse = highest + jnp.log(jnp.sum(jnp.exp(scores - highest[:, None]), axis=-1))
    probs = jnp.exp(scores - lse[:, None])
    probs_low = probs.astype(jnp.bfloat16)
    delta = jnp.sum(grad.astype(jnp.float32) * output.astype(jnp.float32), axis=-1)
    dprobs = jnp.dot(grad, value.T, preferred_element_type=jnp.float32)
    dscores = (probs * (dprobs - delta[:, None])).astype(jnp.bfloat16)
    query_grad = scale * jnp.dot(dscores, key, preferred_element_type=jnp.float32)
    key_grad = scale * jnp.dot(dscores.T, query, preferred_element_type=jnp.float32)
    value_grad = jnp.dot(probs_low.T, grad, preferred_element_type=jnp.float32)
    return (query_grad.astype(jnp.bfloat16), key_grad.astype(jnp.bfloat16), value_grad.astype(jnp.bfloat16))


def split_heads(array):
    return jnp.transpose(array.reshape(array.shape[0], HEADS, HD), (1, 0, 2))


def join_heads(array):
    return jnp.transpose(array, (1, 0, 2)).reshape(array.shape[1], HEADS * HD)


def reference(queries, keys, values, attn_out, out_grad, out_weight, token_sizes):
    head_grad = jnp.dot(out_grad, out_weight.T, preferred_element_type=jnp.float32).astype(jnp.bfloat16)
    bias = jnp.log(token_sizes.astype(jnp.float32)).astype(jnp.bfloat16).astype(jnp.float32)
    count = queries.shape[0]
    biases = jnp.broadcast_to(bias[None, :], (HEADS, count))
    result = lax.map(head_backward, (split_heads(queries), split_heads(keys), split_heads(values), split_heads(head_grad), split_heads(attn_out), biases))
    return (join_heads(result[0]), join_heads(result[1]), join_heads(result[2]))
```

```python
import functools
import math

import jax
import jax.numpy as jnp
from jax import lax
from jax.experimental import pallas as pl
from jax.experimental.pallas import tpu as pltpu
from jax.sharding import PartitionSpec as P

MESH = pl.DeviceIdType.MESH
HD = 128
SCALE = 1.0 / HD**0.5
LOG2E = math.log2(math.e)
BF = jnp.bfloat16
F32 = jnp.float32
NT = (((1,), (1,)), ((), ()))
NN = (((1,), (0,)), ((), ()))
Q, K, V, G, BIAS, DELTA = range(6)
STAT = 6


def dot(a, b, dims):
    return lax.dot_general(a, b, dims, preferred_element_type=F32)


class Place:
    def __init__(self):
        self.c, self.t = lax.axis_index("ctx"), lax.axis_index("tp")
        self.z, self.yh = self.c // 2, self.c % 2
        self.yl, self.x, self.k = self.t // 8, (self.t % 8) // 2, self.t % 2
        self.y = self.yh * 2 + self.yl

    def other(self, d):
        return jnp.logical_or(d[0] != self.c, d[1] != self.t)

    def worker(self, piece, par):
        plane = self.x + 4 * (2 * self.k + par)
        return (plane * 2 + self.yh, (piece // 4) * 8 + (piece % 4) * 2 + self.yl)

    def home(self, s):
        return (s * 2 + self.yh, self.k * 8 + (self.z % 4) * 2 + self.z // 8)

    def along_x(self, j):
        return (self.c, self.yl * 8 + ((self.x + j) % 4) * 2 + self.k)

    def along_y(self, j):
        y = (self.y + j) % 4
        return (self.z * 2 + y // 2, (y % 2) * 8 + self.x * 2 + self.k)

    def chip(self, j):
        return (self.c, ((self.t // 2) ^ j) * 2 + self.k)

    def sibling(self):
        return (self.c, self.t + 1 - 2 * self.k)


def kernel(
    q_ref, k_ref, v_ref, o_ref, og_ref, w_ref, tok_ref, out_ref,
    og, w, qi, ki, vi, oi, gi, brow, dsend,
    qg, kg, vg, gg, bg, dg, st, e, ms, kt, bt, xb,
    dv, dk, dqo, rss, rsr, fin, outs,
    ld, p0s, p0r, a2s, a2r, ags, agr, rs_s, rs_r, ret_s, ret_r,
):
    me = Place()

    loads = [
        pltpu.make_async_copy(og_ref, og.at[:, pl.ds(pl.multiple_of(me.t * 384, 128), 384)], ld.at[0]),
        pltpu.make_async_copy(q_ref, qi, ld.at[1]),
        pltpu.make_async_copy(k_ref, ki, ld.at[2]),
        pltpu.make_async_copy(v_ref, vi, ld.at[3]),
        pltpu.make_async_copy(w_ref, w, ld.at[4]),
        pltpu.make_async_copy(o_ref, oi, ld.at[5]),
    ]
    barrier = pltpu.get_barrier_semaphore()
    partners = [me.home(s) for s in range(16)] + [me.worker(p, r) for p in range(8) for r in range(2)]
    partners += [me.chip(j) for j in range(1, 8)] + [me.sibling()]
    partners += [me.along_y(j) for j in range(1, 4)]
    expected = 0
    for d in partners:
        there = me.other(d)

        @pl.when(there)
        def _():
            pl.semaphore_signal(barrier, inc=1, device_id=d, device_id_type=MESH)

        expected = expected + there.astype(jnp.int32)
    for c in loads:
        c.start()
    brow[...] = jnp.log(tok_ref[...].astype(F32)).astype(BF).astype(F32)
    loads[0].wait()
    pl.semaphore_wait(barrier, expected)

    def remote(src, dst, s, r, d):
        return pltpu.make_async_remote_copy(src, dst, s, r, device_id=d, device_id_type=MESH)

    def og_at(slot):
        return og.at[:, pl.ds(pl.multiple_of(slot * 384, 128), 384)]

    mine = og_at(me.t)
    pushes = [remote(mine, mine, p0s.at[j], p0r.at[me.t], me.chip(j)) for j in range(1, 8)]
    pushes.append(remote(mine, mine, p0s.at[0], p0r.at[me.t], me.sibling()))
    for c in pushes:
        c.start()

    def spread(kind, src_of, dst_of):
        for p in range(8):
            for r in range(2):
                d = me.worker(p, r)
                src, dst = src_of(p, r), dst_of(p)
                send = remote(src, dst, a2s.at[kind, p * 2 + r], a2r.at[kind], d)
                keep = pltpu.make_async_copy(src, dst, a2r.at[kind])
                there = me.other(d)
                pl.when(there)(send.start)
                pl.when(jnp.logical_not(there))(keep.start)

    def spread_done(kind, src_of, dst_of):
        for p in range(8):
            for r in range(2):
                d = me.worker(p, r)
                send = remote(src_of(p, r), dst_of(p), a2s.at[kind, p * 2 + r], a2r.at[kind], d)
                pl.when(me.other(d))(send.wait_send)

    def part(a):
        return lambda p, r: a.at[pl.ds(p * 16, 16), pl.ds(r * 128, 128)]

    def slot_x(a):
        return lambda p: a.at[p % 4, pl.ds(pl.multiple_of(me.z * 16, 16), 16)]

    def slot_y(a):
        return lambda p: a.at[me.yh * 2 + p // 4, pl.ds(pl.multiple_of(me.z * 16, 16), 16)]

    routes = {
        Q: (part(qi), slot_x(qg)),
        K: (part(ki), slot_y(kg)),
        V: (part(vi), slot_y(vg)),
        G: (part(gi), slot_x(gg)),
        BIAS: (lambda p, r: brow, lambda p: bg.at[me.yh * 2 + p // 4, me.z]),
        DELTA: (lambda p, r: dsend.at[p * 2 + r], lambda p: dg.at[p % 4, me.z]),
    }
    for i, kind in ((1, Q), (2, K), (3, V)):
        loads[i].wait()
        spread(kind, *routes[kind])
        if kind == K:
            spread(BIAS, *routes[BIAS])

    acc = jnp.zeros((128, 256), F32)
    loads[4].wait()
    forwards = []
    for n, j in enumerate((0, 1, 3, 4, 5, 7, 2, 6)):
        chip = (me.t // 2) ^ j
        near, far = chip * 2 + me.k, chip * 2 + 1 - me.k
        if j:
            block = og_at(near)
            remote(block, block, p0s.at[0], p0r.at[near], me.sibling()).wait_recv()
            fwd = remote(block, block, p0s.at[8 + j], p0r.at[near], me.sibling())
            fwd.start()
            forwards.append(fwd)
        block = og_at(far)
        remote(block, block, p0s.at[0], p0r.at[far], me.sibling()).wait_recv()
        cols = pl.ds(pl.multiple_of(chip * 768, 128), 768)
        acc = acc + dot(og[:, cols], w[:, cols], NT)
    g = acc.astype(BF)
    gi[...] = g
    spread(G, *routes[G])

    loads[5].wait()
    prod = g.astype(F32) * oi[...].astype(F32)
    lane = lax.broadcasted_iota(jnp.int32, (8, 128), 1)
    keep = (lane // 16) == me.z % 8
    for r in range(2):
        row = jnp.sum(jnp.transpose(prod[:, r * 128 : (r + 1) * 128]), axis=0, keepdims=True)
        rows = pltpu.roll(jnp.broadcast_to(row, (8, 128)), (me.z % 8) * 16, 1)
        for p in range(8):
            turned = pltpu.roll(rows, (128 - p * 16) % 128, 1) if p else rows
            dsend[p * 2 + r] = jnp.where(keep, turned, 0.0)[0:1]
    spread(DELTA, *routes[DELTA])

    def arrived(kind, whole):
        pltpu.make_async_copy(whole, whole, a2r.at[kind]).wait()

    def share(kind, buf, slot, along):
        for j in (1, 3, 2):
            remote(buf.at[slot], buf.at[slot], ags.at[kind, j], agr.at[kind, slot], along(j)).start()

    def shared(kind, buf, slot):
        remote(buf.at[slot], buf.at[slot], ags.at[kind, 0], agr.at[kind, slot], me.sibling()).wait_recv()

    def share_done(kind, buf, slot, along):
        for j in (1, 3, 2):
            remote(buf.at[slot], buf.at[slot], ags.at[kind, j], agr.at[kind, slot], along(j)).wait_send()

    arrived(Q, qg.at[me.x])
    share(Q, qg, me.x, me.along_x)
    arrived(K, kg.at[me.y])
    share(K, kg, me.y, me.along_y)
    arrived(BIAS, bg.at[me.y])
    share(BIAS, bg, me.y, me.along_y)
    arrived(V, vg.at[me.y])
    share(V, vg, me.y, me.along_y)
    for j in (1, 3, 2):
        y = (me.y + j) % 4
        shared(BIAS, bg, y)
        shared(K, kg, y)
    sub = lax.broadcasted_iota(jnp.int32, (16, 128), 0)
    lane = lax.broadcasted_iota(jnp.int32, (16, 128), 1)
    for y in range(4):
        hit = lane == ((y % 2) * 4 + me.x) * 16 + sub
        for s in range(16):
            row = jnp.broadcast_to(bg[y, s], (16, 128))
            xb[pl.ds(y * 256 + s * 16, 16), :] = jnp.where(hit, row, 0.0).astype(BF)
    bt[...] = dot(xb[...], jnp.ones((128, 128), BF), NN) * LOG2E
    for y in range(4):
        kt[:, pl.ds(y * 256, 256)] = jnp.transpose(kg[y].astype(F32)).astype(BF)

    def score(j, carry):
        x = (me.x + j) % 4

        @pl.when(j > 0)
        def _():
            shared(Q, qg, x)

        keys = kg[...].reshape(1024, 128)
        bias = bt[...]
        s = dot(keys, qg[x], NT) * (SCALE * LOG2E) + jnp.concatenate([bias, bias], axis=1)
        m = jnp.max(s, axis=0, keepdims=True)
        p = jnp.exp2(s - m)
        e[x] = p
        ms[x] = m
        st[me.x, x] = m + jnp.log2(jnp.sum(p, axis=0, keepdims=True))
        return carry

    lax.fori_loop(0, 4, score, 0)
    share(STAT, st, me.x, me.along_x)

    arrived(G, gg.at[me.x])
    share(G, gg, me.x, me.along_x)
    arrived(DELTA, dg.at[me.x])
    share(DELTA, dg, me.x, me.along_x)
    for j in (1, 3, 2):
        shared(STAT, st, (me.x + j) % 4)
    for j in (1, 3, 2):
        shared(V, vg, (me.y + j) % 4)

    dv[...] = jnp.zeros_like(dv)
    dk[...] = jnp.zeros_like(dk)

    def grads(j, carry):
        x = (me.x + j) % 4

        @pl.when(j > 0)
        def _():
            shared(G, gg, x)
            shared(DELTA, dg, x)

        parts = [st[i, x] for i in range(4)]
        top = functools.reduce(jnp.maximum, parts)
        lse = top + jnp.log2(sum(jnp.exp2(a - top) for a in parts))
        p = e[x] * jnp.exp2(ms[x] - lse)
        grad = gg[x]
        dv[...] += dot(p.astype(BF), grad, NN)
        delta = jnp.concatenate([jnp.sum(dg[x, 0:8], axis=0), jnp.sum(dg[x, 8:16], axis=0)], axis=1)
        dp = dot(vg[...].reshape(1024, 128), grad, NT)
        ds = (p * (dp - delta)).astype(BF)
        dk[...] += dot(ds, qg[x], NN)
        dq = jnp.transpose(dot(kt[...], ds, NN)) * SCALE

        @pl.when(j == 0)
        def _():
            dqo[...] = dq

        @pl.when(j > 0)
        def _():
            rss[0, x] = dq.astype(BF)
            d = (me.c, me.yl * 8 + x * 2 + me.k)
            remote(rss.at[0, x], rsr.at[0, me.x], rs_s.at[0, x], rs_r.at[0, me.x], d).start()

        return carry

    lax.fori_loop(0, 4, grads, 0)

    for i, total in ((2, dv), (1, dk)):
        for j in (1, 3, 2):
            y = (me.y + j) % 4
            rows = total[pl.ds(pl.multiple_of(y * 256, 256), 256), :]
            rss[i, y] = (rows * SCALE if i == 1 else rows).astype(BF)
            remote(rss.at[i, y], rsr.at[i, me.y], rs_s.at[i, y], rs_r.at[i, me.y], me.along_y(j)).start()

    def give(i, s):
        piece = me.yl * 4 + me.x
        par = (me.z // 4) % 2
        dst = outs.at[
            i, pl.ds(pl.multiple_of(piece * 16, 16), 16), pl.ds(pl.multiple_of(par * 128, 128), 128)
        ]
        src = fin.at[i, pl.ds(s * 16, 16)]
        d = me.home(s)
        return (
            lambda: remote(src, dst, ret_s.at[i, s], ret_r.at[i], d),
            lambda: pltpu.make_async_copy(src, dst, ret_r.at[i]),
            me.other(d),
        )

    for i in (0, 2, 1):
        own = me.x if i == 0 else me.y
        if i == 0:
            total = dqo[...]
        else:
            total = (dv if i == 2 else dk)[pl.ds(pl.multiple_of(me.y * 256, 256), 256), :]
            total = total * SCALE if i == 1 else total
        for j in (1, 3, 2):
            n = (own + j) % 4
            remote(rsr.at[i, n], rsr.at[i, n], rs_s.at[i, 0], rs_r.at[i, n], me.sibling()).wait_recv()
            total = total + rsr[i, n].astype(F32)
        fin[i] = total.astype(BF)
        for s in range(16):
            send, stay, there = give(i, s)
            pl.when(there)(lambda: send().start())
            pl.when(jnp.logical_not(there))(lambda: stay().start())

    for c in pushes + forwards:
        c.wait_send()
    for kind, route in routes.items():
        spread_done(kind, *route)
    for kind, buf, slot, along in (
        (Q, qg, me.x, me.along_x),
        (K, kg, me.y, me.along_y),
        (V, vg, me.y, me.along_y),
        (G, gg, me.x, me.along_x),
        (BIAS, bg, me.y, me.along_y),
        (DELTA, dg, me.x, me.along_x),
        (STAT, st, me.x, me.along_x),
    ):
        share_done(kind, buf, slot, along)
    for i in range(3):
        own = me.x if i == 0 else me.y
        for j in (1, 3, 2):
            n = (own + j) % 4
            remote(rss.at[i, n], rsr.at[i, n], rs_s.at[i, n], rs_r.at[i, n], me.sibling()).wait_send()
        for s in range(16):
            send, stay, there = give(i, s)
            pl.when(there)(lambda: send().wait_send())
        pltpu.make_async_copy(outs.at[i], outs.at[i], ret_r.at[i]).wait()
    out_ref[...] = outs[...]


def split(a_ref, q_ref, k_ref, v_ref):
    q_ref[...] = a_ref[0]
    k_ref[...] = a_ref[1]
    v_ref[...] = a_ref[2]


def local(queries, keys, values, attn_out, out_grad, out_weight, token_sizes):
    any_ = pl.BlockSpec(memory_space=pl.ANY)
    vmem = pl.BlockSpec(memory_space=pltpu.VMEM)
    dma = pltpu.SemaphoreType.DMA
    scratch = [
        pltpu.VMEM((128, 6144), BF),
        pltpu.VMEM((256, 6144), BF),
        pltpu.VMEM((128, 256), BF),
        pltpu.VMEM((128, 256), BF),
        pltpu.VMEM((128, 256), BF),
        pltpu.VMEM((128, 256), BF),
        pltpu.VMEM((128, 256), BF),
        pltpu.VMEM((1, 128), F32),
        pltpu.VMEM((16, 1, 128), F32),
        pltpu.VMEM((4, 256, 128), BF),
        pltpu.VMEM((4, 256, 128), BF),
        pltpu.VMEM((4, 256, 128), BF),
        pltpu.VMEM((4, 256, 128), BF),
        pltpu.VMEM((4, 16, 1, 128), F32),
        pltpu.VMEM((4, 16, 1, 128), F32),
        pltpu.VMEM((4, 4, 1, 256), F32),
        pltpu.VMEM((4, 1024, 256), F32),
        pltpu.VMEM((4, 1, 256), F32),
        pltpu.VMEM((128, 1024), BF),
        pltpu.VMEM((1024, 128), F32),
        pltpu.VMEM((1024, 128), BF),
        pltpu.VMEM((1024, 128), F32),
        pltpu.VMEM((1024, 128), F32),
        pltpu.VMEM((256, 128), F32),
        pltpu.VMEM((3, 4, 256, 128), BF),
        pltpu.VMEM((3, 4, 256, 128), BF),
        pltpu.VMEM((3, 256, 128), BF),
        pltpu.VMEM((3, 128, 256), BF),
        dma((6,)),
        dma((16,)),
        dma((16,)),
        dma((6, 16)),
        dma((6,)),
        dma((7, 4)),
        dma((7, 4)),
        dma((3, 4)),
        dma((3, 4)),
        dma((3, 16)),
        dma((3,)),
    ]
    stacked = pl.pallas_call(
        kernel,
        out_shape=jax.ShapeDtypeStruct((3, 128, 256), BF),
        in_specs=[any_] * 6 + [vmem],
        out_specs=vmem,
        scratch_shapes=scratch,
        compiler_params=pltpu.CompilerParams(
            collective_id=0, has_side_effects=True, vmem_limit_bytes=48 * 2**20
        ),
        cost_estimate=pl.CostEstimate(flops=2 * 10**9, bytes_accessed=4 * 10**6, transcendentals=10**6),
        name="attention_backward",
    )(queries, keys, values, attn_out, out_grad, out_weight, token_sizes.reshape(1, 128))
    shape = jax.ShapeDtypeStruct((128, 256), BF)
    return pl.pallas_call(
        split,
        out_shape=(shape, shape, shape),
        in_specs=[vmem],
        out_specs=(vmem, vmem, vmem),
        name="split_outputs",
    )(stacked)


def solution(mesh):
    rows = P("ctx", "tp")
    return jax.shard_map(
        local,
        mesh=mesh,
        in_specs=(rows, rows, rows, rows, rows, P("tp", None), P("ctx")),
        out_specs=(rows, rows, rows),
        check_vma=False,
    )
```

```python
import functools
import math

import jax
import jax.numpy as jnp
from jax import lax
from jax.experimental import pallas as pl
from jax.experimental.pallas import tpu as pltpu
from jax.sharding import PartitionSpec as P

MESH = pl.DeviceIdType.MESH
HD = 128
SCALE = 1.0 / HD**0.5
LOG2E = math.log2(math.e)
BF = jnp.bfloat16
F32 = jnp.float32
NT = (((1,), (1,)), ((), ()))
NN = (((1,), (0,)), ((), ()))
Q, K, V, G, BIAS, DELTA = range(6)
STAT = 6


def dot(a, b, dims):
    return lax.dot_general(a, b, dims, preferred_element_type=F32)


class Place:
    def __init__(self):
        self.c, self.t = lax.axis_index("ctx"), lax.axis_index("tp")
        self.z, self.yh = self.c // 2, self.c % 2
        self.yl, self.x, self.k = self.t // 8, (self.t % 8) // 2, self.t % 2
        self.y = self.yh * 2 + self.yl

    def other(self, d):
        return jnp.logical_or(d[0] != self.c, d[1] != self.t)

    def worker(self, u):
        return (self.t * 2 + self.yh, u)

    def home(self, s):
        return (s * 2 + self.yh, self.z)

    def group(self, u):
        return (self.c, u)

    def column(self, s):
        return (s * 2 + self.yh, self.t)

    def along_x(self, j):
        return (self.c, self.yl * 8 + ((self.x + j) % 4) * 2 + self.k)

    def along_y(self, j):
        y = (self.y + j) % 4
        return (self.z * 2 + y // 2, (y % 2) * 8 + self.x * 2 + self.k)

    def chip(self, j):
        return (self.c, ((self.t // 2) ^ j) * 2 + self.k)

    def sibling(self):
        return (self.c, self.t + 1 - 2 * self.k)


def kernel(
    q_ref, k_ref, v_ref, o_ref, og_ref, w_ref, tok_ref, out_ref,
    og, w, qi, ki, vi, oi, gi, brow, dsend, relay, drelay,
    qg, kg, vg, gg, bg, dg, st, e, ms, kt, bt, xb,
    dv, dk, dqo, rss, rsr, fin, outs,
    ld, p0s, p0r, rls, rlr, a2s, a2r, ags, agr, rs_s, rs_r, ret_s, ret_r,
):
    me = Place()

    drains, pend = [], {}

    def finish():
        for wait in list(pend.values()) + drains:
            wait()
        out_ref[...] = outs[...]

    def remote(src, dst, s, r, d):
        return pltpu.make_async_remote_copy(src, dst, s, r, device_id=d, device_id_type=MESH)

    def landed(buf, sem):
        return lambda: pltpu.make_async_copy(buf, buf, sem).wait()

    def start(c):
        c.start()
        drains.append(c.wait_send)

    barrier = pltpu.get_barrier_semaphore()
    far = (8, 7, 9, 6, 10, 5, 11, 4, 12, 3, 13, 2, 14, 1, 15, 0)
    partners = [me.column((me.z + j) % 16) for j in far] + [me.home((me.z + j) % 16) for j in far]
    partners += [me.worker(u) for u in range(16)] + [me.group(u) for u in range(16)]
    partners += [(me.z * 2 + 1 - me.yh, l * 8 + me.x * 2 + me.k) for l in range(2)]
    expected = 0
    for d in partners:
        there = me.other(d)

        @pl.when(there)
        def _():
            pl.semaphore_signal(barrier, inc=1, device_id=d, device_id_type=MESH)

        expected = expected + there.astype(jnp.int32)

    def og_at(slot):
        return og.at[:, pl.ds(pl.multiple_of(slot * 384, 128), 384)]

    mine = og_at(me.t)
    loads = [
        pltpu.make_async_copy(src, dst, ld.at[i])
        for i, (src, dst) in enumerate(
            ((og_ref, mine), (q_ref, qi), (k_ref, ki), (v_ref, vi), (w_ref, w), (o_ref, oi))
        )
    ]
    for i, c in enumerate(loads):
        c.start()
        pend["load", i] = c.wait

    def loaded(i):
        pend.pop(("load", i))()

    brow[...] = jnp.log(tok_ref[...].astype(F32)).astype(BF).astype(F32)
    loaded(0)
    pl.semaphore_wait(barrier, expected)

    def send(src, dst, ss, rs, d):
        there = me.other(d)
        c = remote(src, dst, ss, rs, d)
        pl.when(there)(lambda: c.start())
        pl.when(jnp.logical_not(there))(lambda: pltpu.make_async_copy(src, dst, rs).start())
        drains.append(lambda: pl.when(there)(lambda: c.wait_send()))

    def part(a):
        return lambda u: a.at[pl.ds((u // 8 * 4 + u % 8 // 2) * 16, 16), pl.ds((u % 2) * 128, 128)]

    here = pl.ds(pl.multiple_of(me.z * 16, 16), 16)
    routes = {
        Q: (part(qi), relay.at[0], qg.at[me.x, here], qg.at[me.x]),
        K: (part(ki), relay.at[1], kg.at[me.y, here], kg.at[me.y]),
        V: (part(vi), relay.at[2], vg.at[me.y, here], vg.at[me.y]),
        G: (part(gi), relay.at[3], gg.at[me.x, here], gg.at[me.x]),
        DELTA: (lambda u: dsend.at[u], drelay, dg.at[me.x, me.z], dg.at[me.x]),
        BIAS: (None, None, bg.at[me.y, me.z], bg.at[me.y]),
    }

    def spread(kind):
        src, mid, _, _ = routes[kind]
        for u in range(16):
            send(src(u), mid.at[me.t], rls.at[kind, u], rlr.at[kind], me.group(u))
        pend["relay", kind] = landed(mid, rlr.at[kind])

    def climb(kind):
        _, mid, dst, whole = routes[kind]
        if mid is not None:
            pend.pop(("relay", kind))()
        for s in range(16):
            src = brow if mid is None else mid.at[s]
            send(src, dst, a2s.at[kind, s], a2r.at[kind], me.column(s))
        pend["a2a", kind] = landed(whole, a2r.at[kind])

    def arrived(kind):
        pend.pop(("a2a", kind))()

    for i, kind in ((1, Q), (2, K)):
        loaded(i)
        spread(kind)

    for j in range(1, 8):
        start(remote(mine, mine, p0s.at[j], p0r.at[me.t], me.chip(j)))
    start(remote(mine, mine, p0s.at[0], p0r.at[me.t], me.sibling()))
    for j in range(8):
        near = ((me.t // 2) ^ j) * 2 + me.k
        if j:
            pend["og", j] = landed(og_at(near), p0r.at[near])
        else:
            far = near + 1 - 2 * me.k
            pend["og", j] = landed(og_at(far), p0r.at[far])
    climb(BIAS)
    loaded(3)
    spread(V)
    climb(Q)
    climb(K)

    loaded(4)
    for key in [key for key in pend if key[0] == "og"]:
        del pend[key]
    acc = jnp.zeros((128, 256), F32)
    for j in (0, 1, 3, 4, 5, 7, 2, 6):
        chip = (me.t // 2) ^ j
        near, far = chip * 2 + me.k, chip * 2 + 1 - me.k
        if j:
            block = og_at(near)
            landed(block, p0r.at[near])()
            start(remote(block, block, p0s.at[8 + j], p0r.at[near], me.sibling()))
        landed(og_at(far), p0r.at[far])()
        cols = pl.ds(pl.multiple_of(chip * 768, 128), 768)
        acc = acc + dot(og[:, cols], w[:, cols], NT)
    g = acc.astype(BF)
    gi[...] = g
    spread(G)
    climb(V)
    climb(G)

    loaded(5)
    prod = g.astype(F32) * oi[...].astype(F32)
    lane = lax.broadcasted_iota(jnp.int32, (8, 128), 1)
    keep = (lane // 16) == me.z % 8
    for r in range(2):
        row = jnp.sum(jnp.transpose(prod[:, r * 128 : (r + 1) * 128]), axis=0, keepdims=True)
        rows = pltpu.roll(jnp.broadcast_to(row, (8, 128)), (me.z % 8) * 16, 1)
        for p in range(8):
            turned = pltpu.roll(rows, (128 - p * 16) % 128, 1) if p else rows
            dsend[p // 4 * 8 + p % 4 * 2 + r] = jnp.where(keep, turned, 0.0)[0:1]
    spread(DELTA)
    climb(DELTA)

    def share(kind, buf, own, along):
        for j in (1, 3, 2):
            start(remote(buf.at[own], buf.at[own], ags.at[kind, j], agr.at[kind, own], along(j)))
            n = (own + j) % 4
            pend["ag", kind, j] = landed(buf.at[n], agr.at[kind, n])

    def shared(kind):
        for j in (1, 3, 2):
            pend.pop(("ag", kind, j))()

    arrived(Q)
    share(Q, qg, me.x, me.along_x)
    arrived(K)
    share(K, kg, me.y, me.along_y)
    arrived(BIAS)
    share(BIAS, bg, me.y, me.along_y)
    arrived(V)
    share(V, vg, me.y, me.along_y)
    shared(BIAS)
    shared(K)
    sub = lax.broadcasted_iota(jnp.int32, (16, 128), 0)
    lane = lax.broadcasted_iota(jnp.int32, (16, 128), 1)
    for y in range(4):
        hit = lane == ((y % 2) * 4 + me.x) * 16 + sub
        for s in range(16):
            row = jnp.broadcast_to(bg[y, s], (16, 128))
            xb[pl.ds(y * 256 + s * 16, 16), :] = jnp.where(hit, row, 0.0).astype(BF)
    bt[...] = dot(xb[...], jnp.ones((128, 128), BF), NN) * LOG2E
    for y in range(4):
        kt[:, pl.ds(y * 256, 256)] = jnp.transpose(kg[y].astype(F32)).astype(BF)
    shared(Q)

    def score(j, carry):
        x = (me.x + j) % 4
        keys = kg[...].reshape(1024, 128)
        bias = bt[...]
        s = dot(keys, qg[x], NT) * (SCALE * LOG2E) + jnp.concatenate([bias, bias], axis=1)
        m = jnp.max(s, axis=0, keepdims=True)
        p = jnp.exp2(s - m)
        e[x] = p
        ms[x] = m
        st[me.x, x] = m + jnp.log2(jnp.sum(p, axis=0, keepdims=True))
        return carry

    lax.fori_loop(0, 4, score, 0)
    share(STAT, st, me.x, me.along_x)

    arrived(G)
    share(G, gg, me.x, me.along_x)
    arrived(DELTA)
    share(DELTA, dg, me.x, me.along_x)
    shared(STAT)
    shared(V)
    shared(G)
    shared(DELTA)

    dv[...] = jnp.zeros_like(dv)
    dk[...] = jnp.zeros_like(dk)

    def to_sum(i, own, n, d):
        return remote(rss.at[i, n], rsr.at[i, own], rs_s.at[i, n], rs_r.at[i, own], d)

    def grads(j, carry):
        x = (me.x + j) % 4
        parts = [st[i, x] for i in range(4)]
        top = functools.reduce(jnp.maximum, parts)
        lse = top + jnp.log2(sum(jnp.exp2(a - top) for a in parts))
        p = e[x] * jnp.exp2(ms[x] - lse)
        grad = gg[x]
        dv[...] += dot(p.astype(BF), grad, NN)
        delta = jnp.concatenate([jnp.sum(dg[x, 0:8], axis=0), jnp.sum(dg[x, 8:16], axis=0)], axis=1)
        dp = dot(vg[...].reshape(1024, 128), grad, NT)
        ds = (p * (dp - delta)).astype(BF)
        dk[...] += dot(ds, qg[x], NN)
        dq = jnp.transpose(dot(kt[...], ds, NN)) * SCALE

        @pl.when(j == 0)
        def _():
            dqo[...] = dq

        @pl.when(j > 0)
        def _():
            rss[0, x] = dq.astype(BF)
            to_sum(0, me.x, x, (me.c, me.yl * 8 + x * 2 + me.k)).start()

        return carry

    lax.fori_loop(0, 4, grads, 0)
    for i, own in ((0, me.x), (1, me.y), (2, me.y)):
        for j in (1, 3, 2):
            n = (own + j) % 4
            if i == 0:
                drains.append(to_sum(i, own, n, me.sibling()).wait_send)
                pend["rs", i, j] = landed(rsr.at[i, n], rs_r.at[i, n])

    for i, total in ((2, dv), (1, dk)):
        for j in (1, 3, 2):
            y = (me.y + j) % 4
            rows = total[pl.ds(pl.multiple_of(y * 256, 256), 256), :]
            rss[i, y] = (rows * SCALE if i == 1 else rows).astype(BF)
            start(to_sum(i, me.y, y, me.along_y(j)))
            pend["rs", i, j] = landed(rsr.at[i, y], rs_r.at[i, y])

    def give(i, act, act_self):
        piece = me.yl * 4 + me.x
        dst = outs.at[
            i, pl.ds(pl.multiple_of(piece * 16, 16), 16), pl.ds(pl.multiple_of(me.k * 128, 128), 128)
        ]
        for s in range(16):
            src = fin.at[i, pl.ds(s * 16, 16)]
            d = me.home(s)
            there = me.other(d)
            pl.when(there)(lambda: act(remote(src, dst, ret_s.at[i, s], ret_r.at[i], d)))
            if act_self:
                pl.when(jnp.logical_not(there))(lambda: pltpu.make_async_copy(src, dst, ret_r.at[i]).start())

    for i in (0, 2, 1):
        own = me.x if i == 0 else me.y
        if i == 0:
            total = dqo[...]
        else:
            total = (dv if i == 2 else dk)[pl.ds(pl.multiple_of(me.y * 256, 256), 256), :]
            total = total * SCALE if i == 1 else total
        for j in (1, 3, 2):
            pend.pop(("rs", i, j))()
            total = total + rsr[i, (own + j) % 4].astype(F32)
        fin[i] = total.astype(BF)
        give(i, lambda c: c.start(), True)
        drains.append(functools.partial(give, i, lambda c: c.wait_send(), False))
        pend["ret", i] = landed(outs.at[i], ret_r.at[i])
    finish()


def split(a_ref, q_ref, k_ref, v_ref, a, into, out):
    outs = (q_ref, k_ref, v_ref)
    first = [pltpu.make_async_copy(a_ref.at[i], a.at[i], into.at[i]) for i in range(3)]
    then = [pltpu.make_async_copy(a.at[i], outs[i], out.at[i]) for i in range(3)]
    for c in first:
        c.start()
    for c, d in zip(first, then):
        c.wait()
        d.start()
    for d in then:
        d.wait()


def local(queries, keys, values, attn_out, out_grad, out_weight, token_sizes):
    any_ = pl.BlockSpec(memory_space=pl.ANY)
    vmem = pl.BlockSpec(memory_space=pltpu.VMEM)
    dma = pltpu.SemaphoreType.DMA
    scratch = [
        pltpu.VMEM((128, 6144), BF),
        pltpu.VMEM((256, 6144), BF),
        pltpu.VMEM((128, 256), BF),
        pltpu.VMEM((128, 256), BF),
        pltpu.VMEM((128, 256), BF),
        pltpu.VMEM((128, 256), BF),
        pltpu.VMEM((128, 256), BF),
        pltpu.VMEM((1, 128), F32),
        pltpu.VMEM((16, 1, 128), F32),
        pltpu.VMEM((4, 16, 16, 128), BF),
        pltpu.VMEM((16, 1, 128), F32),
        pltpu.VMEM((4, 256, 128), BF),
        pltpu.VMEM((4, 256, 128), BF),
        pltpu.VMEM((4, 256, 128), BF),
        pltpu.VMEM((4, 256, 128), BF),
        pltpu.VMEM((4, 16, 1, 128), F32),
        pltpu.VMEM((4, 16, 1, 128), F32),
        pltpu.VMEM((4, 4, 1, 256), F32),
        pltpu.VMEM((4, 1024, 256), F32),
        pltpu.VMEM((4, 1, 256), F32),
        pltpu.VMEM((128, 1024), BF),
        pltpu.VMEM((1024, 128), F32),
        pltpu.VMEM((1024, 128), BF),
        pltpu.VMEM((1024, 128), F32),
        pltpu.VMEM((1024, 128), F32),
        pltpu.VMEM((256, 128), F32),
        pltpu.VMEM((3, 4, 256, 128), BF),
        pltpu.VMEM((3, 4, 256, 128), BF),
        pltpu.VMEM((3, 256, 128), BF),
        pltpu.VMEM((3, 128, 256), BF),
        dma((6,)),
        dma((16,)),
        dma((16,)),
        dma((6, 16)),
        dma((6,)),
        dma((6, 16)),
        dma((6,)),
        dma((7, 4)),
        dma((7, 4)),
        dma((3, 4)),
        dma((3, 4)),
        dma((3, 16)),
        dma((3,)),
    ]
    stacked = pl.pallas_call(
        kernel,
        out_shape=jax.ShapeDtypeStruct((3, 128, 256), BF),
        in_specs=[any_] * 6 + [vmem],
        out_specs=vmem,
        scratch_shapes=scratch,
        compiler_params=pltpu.CompilerParams(
            collective_id=0, has_side_effects=True, vmem_limit_bytes=62 * 2**20
        ),
        cost_estimate=pl.CostEstimate(flops=2 * 10**9, bytes_accessed=4 * 10**6, transcendentals=10**6),
        name="attention_backward",
    )(queries, keys, values, attn_out, out_grad, out_weight, token_sizes.reshape(1, 128))
    shape = jax.ShapeDtypeStruct((128, 256), BF)
    return pl.pallas_call(
        split,
        out_shape=(shape, shape, shape),
        in_specs=[any_],
        out_specs=(any_, any_, any_),
        scratch_shapes=[pltpu.VMEM((3, 128, 256), BF), dma((3,)), dma((3,))],
        compiler_params=pltpu.CompilerParams(vmem_limit_bytes=62 * 2**20),
        name="split_outputs",
    )(stacked)


def solution(mesh):
    rows = P("ctx", "tp")
    return jax.shard_map(
        local,
        mesh=mesh,
        in_specs=(rows, rows, rows, rows, rows, P("tp", None), P("ctx")),
        out_specs=(rows, rows, rows),
        check_vma=False,
    )
```

```python
import functools
import math

import jax
import jax.numpy as jnp
from jax import lax
from jax.experimental import pallas as pl
from jax.experimental.pallas import tpu as pltpu
from jax.sharding import PartitionSpec as P

MESH = pl.DeviceIdType.MESH
HD = 128
SCALE = 1.0 / HD**0.5
LOG2E = math.log2(math.e)
BF = jnp.bfloat16
F32 = jnp.float32
NT = (((1,), (1,)), ((), ()))
NN = (((1,), (0,)), ((), ()))
Q, K, V, G, BIAS, DELTA = range(6)
STAT = 6


def each(count, body):
    lax.fori_loop(0, count, lambda i, c: (body(i), c)[1], 0)


def dot(a, b, dims):
    return lax.dot_general(a, b, dims, preferred_element_type=F32)


class Place:
    def __init__(self):
        self.c, self.t = lax.axis_index("ctx"), lax.axis_index("tp")
        self.z, self.yh = self.c // 2, self.c % 2
        self.yl, self.x, self.k = self.t // 8, (self.t % 8) // 2, self.t % 2
        self.y = self.yh * 2 + self.yl

    def other(self, d):
        return jnp.logical_or(d[0] != self.c, d[1] != self.t)

    def worker(self, u):
        return (self.t * 2 + self.yh, u)

    def home(self, s):
        return (s * 2 + self.yh, self.z)

    def group(self, u):
        return (self.c, u)

    def column(self, s):
        return (s * 2 + self.yh, self.t)

    def along_x(self, j):
        return (self.c, self.yl * 8 + ((self.x + j) % 4) * 2 + self.k)

    def along_y(self, j):
        y = (self.y + j) % 4
        return (self.z * 2 + y // 2, (y % 2) * 8 + self.x * 2 + self.k)

    def chip(self, j):
        return (self.c, ((self.t // 2) ^ j) * 2 + self.k)

    def sibling(self):
        return (self.c, self.t + 1 - 2 * self.k)


def kernel(
    q_ref, k_ref, v_ref, o_ref, og_ref, w_ref, tok_ref, out_ref,
    og, w, qi, ki, vi, oi, gi, brow, drow, dsend, relay, drelay,
    qg, kg, vg, gg, bg, dg, st, e, ms, kt, bt, xb,
    dv, dk, dqo, rss, rsr, fin, outs,
    word, ld, p0s, p0r, rls, rlr, a2s, a2r, ags, agr, rs_s, rs_r, ret_s, ret_r,
):
    me = Place()

    drains, pend = [], {}

    def finish():
        for wait in list(pend.values()) + drains:
            wait()
        out_ref[...] = outs[...]

    def remote(src, dst, s, r, d):
        return pltpu.make_async_remote_copy(src, dst, s, r, device_id=d, device_id_type=MESH)

    def landed(buf, sem):
        return lambda: pltpu.make_async_copy(buf, buf, sem).wait()

    barrier = pltpu.get_barrier_semaphore()

    def greet(d):
        pl.semaphore_signal(barrier, inc=1, device_id=d, device_id_type=MESH)

    each(15, lambda i: greet(me.group((me.t + i + 1) % 16)))
    for l in range(2):
        greet((me.z * 2 + 1 - me.yh, l * 8 + me.x * 2 + me.k))
    for j in (1, 15):
        greet(me.column((me.z + j) % 16))
    expected = 19
    apart = me.t != me.z

    def tell(step):
        for j in (2**step, 16 - 2**step):
            d = me.column((me.z + j) % 16)
            pl.semaphore_signal(word.at[step], inc=1, device_id=d, device_id_type=MESH)

    def told(step):
        pl.semaphore_wait(word.at[step], 2)

    def og_at(slot):
        return og.at[:, pl.ds(pl.multiple_of(slot * 384, 128), 384)]

    mine = og_at(me.t)
    loads = [
        pltpu.make_async_copy(src, dst, ld.at[i])
        for i, (src, dst) in enumerate(
            ((og_ref, mine), (q_ref, qi), (k_ref, ki), (v_ref, vi), (w_ref, w), (o_ref, oi))
        )
    ]
    for i, c in enumerate(loads):
        c.start()
        pend["load", i] = c.wait

    def loaded(i):
        pend.pop(("load", i))()

    brow[...] = jnp.log(tok_ref[...].astype(F32)).astype(BF).astype(F32)
    loaded(0)
    pl.semaphore_wait(barrier, expected)
    tell(0)

    def part(a):
        return lambda u: a.at[pl.ds(pl.multiple_of((u // 8 * 4 + u % 8 // 2) * 16, 16), 16), pl.ds(pl.multiple_of((u % 2) * 128, 128), 128)]

    here = pl.ds(pl.multiple_of(me.z * 16, 16), 16)
    routes = {
        Q: (part(qi), relay.at[0], qg.at[me.x, here], qg.at[me.x]),
        K: (part(ki), relay.at[1], kg.at[me.y, here], kg.at[me.y]),
        V: (part(vi), relay.at[2], vg.at[me.y, here], vg.at[me.y]),
        G: (part(gi), relay.at[3], gg.at[me.x, here], gg.at[me.x]),
        DELTA: (lambda u: dsend.at[u], drelay, dg.at[me.x, me.z], dg.at[me.x]),
        BIAS: (None, None, bg.at[me.y, me.z], bg.at[me.y]),
    }

    def spread(kind):
        src, mid, _, _ = routes[kind]
        pltpu.make_async_copy(src(me.t), mid.at[me.t], rlr.at[kind]).start()

        def one(i):
            u = (me.t + i + 1) % 16
            remote(src(u), mid.at[me.t], rls.at[kind], rlr.at[kind], me.group(u)).start()

        each(15, one)
        drains.append(landed(mid.at[0:15], rls.at[kind]))
        pend["relay", kind] = landed(mid, rlr.at[kind])

    def climb(kind):
        _, mid, dst, whole = routes[kind]
        src = (lambda s: brow) if mid is None else (lambda s: mid.at[s])
        if mid is not None:
            pend.pop(("relay", kind))()
        pltpu.make_async_copy(src(me.z), dst, a2r.at[kind]).start()

        def one(i):
            s = (me.z + 1 + (i + 7) % 15) % 16
            remote(src(s), dst, a2s.at[kind], a2r.at[kind], me.column(s)).start()

        each(15, one)
        sent = bg.at[0, 0:15] if mid is None else mid.at[0:15]
        drains.append(landed(sent, a2s.at[kind]))
        pend["a2a", kind] = landed(whole, a2r.at[kind])

    def arrived(kind):
        pend.pop(("a2a", kind))()

    for i, kind in ((1, Q), (2, K)):
        loaded(i)
        spread(kind)

    def push(i):
        remote(mine, mine, p0s.at[0], p0r.at[me.t], me.chip(i + 1)).start()

    each(7, push)
    remote(mine, mine, p0s.at[0], p0r.at[me.t], me.sibling()).start()
    drains.append(landed(og.at[:, 0:3072], p0s.at[0]))
    sib = me.t + 1 - 2 * me.k
    pend["og", 0] = landed(og_at(sib), p0r.at[sib])

    def pushed(i):
        near = ((me.t // 2) ^ (i + 1)) * 2 + me.k
        landed(og_at(near), p0r.at[near])()

    pend["og", 1] = lambda: each(7, pushed)
    loaded(3)
    spread(V)
    told(0)
    tell(1)
    told(1)
    tell(2)
    told(2)
    climb(BIAS)
    climb(Q)
    climb(K)

    loaded(4)
    for key in [key for key in pend if key[0] == "og"]:
        del pend[key]
    def features(chip):
        cols = pl.ds(pl.multiple_of(chip * 768, 128), 768)
        return dot(og[:, cols], w[:, cols], NT)

    landed(og_at(sib), p0r.at[sib])()

    def gather(i, acc):
        chip = (me.t // 2) ^ (i + 1)
        near, far = chip * 2 + me.k, chip * 2 + 1 - me.k
        block = og_at(near)
        landed(block, p0r.at[near])()
        remote(block, block, p0s.at[1], p0r.at[near], me.sibling()).start()
        landed(og_at(far), p0r.at[far])()
        return acc + features(chip)

    acc = lax.fori_loop(0, 7, gather, features(me.t // 2))
    drains.append(landed(og.at[:, 0:2688], p0s.at[1]))
    g = acc.astype(BF)
    gi[...] = g
    spread(G)

    loaded(5)
    prod = g.astype(F32) * oi[...].astype(F32)
    lane = lax.broadcasted_iota(jnp.int32, (8, 128), 1)
    keep = (lane // 16) == me.z % 8
    for r in range(2):
        row = jnp.sum(jnp.transpose(prod[:, r * 128 : (r + 1) * 128]), axis=0, keepdims=True)
        drow[r] = jnp.broadcast_to(row, (8, 128))

    def lay(u):
        piece = u // 8 * 4 + u % 8 // 2
        rows = pltpu.roll(drow[u % 2], (me.z * 16 - piece * 16 + 256) % 128, 1)
        dsend[u] = jnp.where(keep, rows, 0.0)[0:1]

    each(16, lay)
    spread(DELTA)
    climb(V)
    climb(G)
    climb(DELTA)

    def share(kind, buf, own, along):
        def one(i):
            remote(buf.at[own], buf.at[own], ags.at[kind], agr.at[kind, own], along(i + 1)).start()

        def wait(i):
            n = (own + i + 1) % 4
            landed(buf.at[n], agr.at[kind, n])()

        each(3, one)
        drains.append(landed(buf.at[0:3], ags.at[kind]))
        pend["ag", kind] = lambda: each(3, wait)

    def shared(kind):
        pend.pop(("ag", kind))()

    arrived(Q)
    share(Q, qg, me.x, me.along_x)
    arrived(K)
    share(K, kg, me.y, me.along_y)
    arrived(BIAS)
    share(BIAS, bg, me.y, me.along_y)
    arrived(V)
    share(V, vg, me.y, me.along_y)
    shared(BIAS)
    shared(K)
    sub = lax.broadcasted_iota(jnp.int32, (16, 128), 0)
    lane = lax.broadcasted_iota(jnp.int32, (16, 128), 1)

    def bias_rows(i):
        hit = lane == ((i // 16 % 2) * 4 + me.x) * 16 + sub
        row = jnp.broadcast_to(bg[i // 16, i % 16], (16, 128))
        xb[pl.ds(pl.multiple_of(i * 16, 16), 16), :] = jnp.where(hit, row, 0.0).astype(BF)

    each(64, bias_rows)
    bt[...] = dot(xb[...], jnp.ones((128, 128), BF), NN) * LOG2E

    def turn(y):
        kt[:, pl.ds(pl.multiple_of(y * 256, 256), 256)] = jnp.transpose(kg[y].astype(F32)).astype(BF)

    each(4, turn)
    shared(Q)

    def score(j, carry):
        x = (me.x + j) % 4
        keys = kg[...].reshape(1024, 128)
        bias = bt[...]
        s = dot(keys, qg[x], NT) * (SCALE * LOG2E) + jnp.concatenate([bias, bias], axis=1)
        m = jnp.max(s, axis=0, keepdims=True)
        p = jnp.exp2(s - m)
        e[x] = p
        ms[x] = m
        st[me.x, x] = m + jnp.log2(jnp.sum(p, axis=0, keepdims=True))
        return carry

    lax.fori_loop(0, 4, score, 0)
    share(STAT, st, me.x, me.along_x)

    arrived(G)
    share(G, gg, me.x, me.along_x)
    arrived(DELTA)
    share(DELTA, dg, me.x, me.along_x)
    shared(STAT)

    dv[...] = jnp.zeros_like(dv)
    dk[...] = jnp.zeros_like(dk)

    def to_sum(i, own, n, d):
        return remote(rss.at[i, n], rsr.at[i, own], rs_s.at[i], rs_r.at[i, own], d)

    def summed(i, own):
        def wait(j):
            n = (own + j + 1) % 4
            landed(rsr.at[i, n], rs_r.at[i, n])()

        drains.append(landed(rss.at[i, 0:3], rs_s.at[i]))
        pend["rs", i] = lambda: each(3, wait)

    def push_sums(i, total):
        def one(j):
            y = (me.y + j + 1) % 4
            rows = total[pl.ds(pl.multiple_of(y * 256, 256), 256), :]
            rss[i, y] = (rows * SCALE if i == 1 else rows).astype(BF)
            to_sum(i, me.y, y, me.along_y(j + 1)).start()

        each(3, one)
        summed(i, me.y)

    pend.pop(("ag", G))

    def weigh(j, carry):
        x = (me.x + (j ^ (j // 2))) % 4
        pl.when(j > 0)(landed(gg.at[x], agr.at[G, x]))
        parts = [st[i, x] for i in range(4)]
        top = functools.reduce(jnp.maximum, parts)
        lse = top + jnp.log2(sum(jnp.exp2(a - top) for a in parts))
        p = e[x] * jnp.exp2(ms[x] - lse)
        e[x] = p
        dv[...] += dot(p.astype(BF), gg[x], NN)
        return carry

    lax.fori_loop(0, 4, weigh, 0)
    push_sums(2, dv)
    shared(DELTA)
    shared(V)

    def grads(j, carry):
        x = (me.x + 1 + j) % 4
        delta = jnp.concatenate([jnp.sum(dg[x, 0:8], axis=0), jnp.sum(dg[x, 8:16], axis=0)], axis=1)
        dp = dot(vg[...].reshape(1024, 128), gg[x], NT)
        ds = (e[x] * (dp - delta)).astype(BF)
        dk[...] += dot(ds, qg[x], NN)
        dq = jnp.transpose(dot(kt[...], ds, NN)) * SCALE

        @pl.when(j == 3)
        def _():
            dqo[...] = dq

        @pl.when(j < 3)
        def _():
            rss[0, x] = dq.astype(BF)
            to_sum(0, me.x, x, (me.c, me.yl * 8 + x * 2 + me.k)).start()

        return carry

    lax.fori_loop(0, 4, grads, 0)
    summed(0, me.x)
    push_sums(1, dk)

    def give(i):
        piece = me.yl * 4 + me.x
        dst = outs.at[
            i, pl.ds(pl.multiple_of(piece * 16, 16), 16), pl.ds(pl.multiple_of(me.k * 128, 128), 128)
        ]

        def src(s):
            return fin.at[i, pl.ds(pl.multiple_of(s * 16, 16), 16)]

        def one(j):
            s = (me.z + 1 + (j + 7) % 15) % 16
            remote(src(s), dst, ret_s.at[i, 0], ret_r.at[i], me.home(s)).start()

        each(15, one)
        last = remote(src(me.z), dst, ret_s.at[i, 1], ret_r.at[i], me.home(me.z))
        pl.when(apart)(lambda: last.start())
        pl.when(jnp.logical_not(apart))(lambda: pltpu.make_async_copy(src(me.z), dst, ret_r.at[i]).start())
        drains.append(landed(fin.at[i, 0:240], ret_s.at[i, 0]))
        drains.append(lambda: pl.when(apart)(lambda: last.wait_send()))
        pend["ret", i] = landed(outs.at[i], ret_r.at[i])

    for i in (2, 0, 1):
        own = me.x if i == 0 else me.y
        if i == 0:
            total = dqo[...]
        else:
            total = (dv if i == 2 else dk)[pl.ds(pl.multiple_of(me.y * 256, 256), 256), :]
            total = total * SCALE if i == 1 else total
        pend.pop(("rs", i))()
        for j in (1, 3, 2):
            total = total + rsr[i, (own + j) % 4].astype(F32)
        fin[i] = total.astype(BF)
        give(i)
    finish()


def split(a_ref, q_ref, k_ref, v_ref, a, into, out):
    outs = (q_ref, k_ref, v_ref)
    first = [pltpu.make_async_copy(a_ref.at[i], a.at[i], into.at[i]) for i in range(3)]
    then = [pltpu.make_async_copy(a.at[i], outs[i], out.at[i]) for i in range(3)]
    for c in first:
        c.start()
    for c, d in zip(first, then):
        c.wait()
        d.start()
    for d in then:
        d.wait()


def local(queries, keys, values, attn_out, out_grad, out_weight, token_sizes):
    any_ = pl.BlockSpec(memory_space=pl.ANY)
    vmem = pl.BlockSpec(memory_space=pltpu.VMEM)
    dma = pltpu.SemaphoreType.DMA
    scratch = [
        pltpu.VMEM((128, 6144), BF),
        pltpu.VMEM((256, 6144), BF),
        pltpu.VMEM((128, 256), BF),
        pltpu.VMEM((128, 256), BF),
        pltpu.VMEM((128, 256), BF),
        pltpu.VMEM((128, 256), BF),
        pltpu.VMEM((128, 256), BF),
        pltpu.VMEM((1, 128), F32),
        pltpu.VMEM((2, 8, 128), F32),
        pltpu.VMEM((16, 1, 128), F32),
        pltpu.VMEM((4, 16, 16, 128), BF),
        pltpu.VMEM((16, 1, 128), F32),
        pltpu.VMEM((4, 256, 128), BF),
        pltpu.VMEM((4, 256, 128), BF),
        pltpu.VMEM((4, 256, 128), BF),
        pltpu.VMEM((4, 256, 128), BF),
        pltpu.VMEM((4, 16, 1, 128), F32),
        pltpu.VMEM((4, 16, 1, 128), F32),
        pltpu.VMEM((4, 4, 1, 256), F32),
        pltpu.VMEM((4, 1024, 256), F32),
        pltpu.VMEM((4, 1, 256), F32),
        pltpu.VMEM((128, 1024), BF),
        pltpu.VMEM((1024, 128), F32),
        pltpu.VMEM((1024, 128), BF),
        pltpu.VMEM((1024, 128), F32),
        pltpu.VMEM((1024, 128), F32),
        pltpu.VMEM((256, 128), F32),
        pltpu.VMEM((3, 4, 256, 128), BF),
        pltpu.VMEM((3, 4, 256, 128), BF),
        pltpu.VMEM((3, 256, 128), BF),
        pltpu.VMEM((3, 128, 256), BF),
        pltpu.SemaphoreType.REGULAR((3,)),
        dma((6,)),
        dma((2,)),
        dma((16,)),
        dma((6,)),
        dma((6,)),
        dma((6,)),
        dma((6,)),
        dma((7,)),
        dma((7, 4)),
        dma((3,)),
        dma((3, 4)),
        dma((3, 2)),
        dma((3,)),
    ]
    stacked = pl.pallas_call(
        kernel,
        out_shape=jax.ShapeDtypeStruct((3, 128, 256), BF),
        in_specs=[any_] * 6 + [vmem],
        out_specs=vmem,
        scratch_shapes=scratch,
        compiler_params=pltpu.CompilerParams(
            collective_id=0, has_side_effects=True, vmem_limit_bytes=62 * 2**20
        ),
        cost_estimate=pl.CostEstimate(flops=2 * 10**9, bytes_accessed=4 * 10**6, transcendentals=10**6),
        name="attention_backward",
    )(queries, keys, values, attn_out, out_grad, out_weight, token_sizes.reshape(1, 128))
    shape = jax.ShapeDtypeStruct((128, 256), BF)
    return pl.pallas_call(
        split,
        out_shape=(shape, shape, shape),
        in_specs=[any_],
        out_specs=(any_, any_, any_),
        scratch_shapes=[pltpu.VMEM((3, 128, 256), BF), dma((3,)), dma((3,))],
        compiler_params=pltpu.CompilerParams(vmem_limit_bytes=62 * 2**20),
        name="split_outputs",
    )(stacked)


def solution(mesh):
    rows = P("ctx", "tp")
    return jax.shard_map(
        local,
        mesh=mesh,
        in_specs=(rows, rows, rows, rows, rows, P("tp", None), P("ctx")),
        out_specs=(rows, rows, rows),
        check_vma=False,
    )
```

```python
import functools
import math

import jax
import jax.numpy as jnp
from jax import lax
from jax.experimental import pallas as pl
from jax.experimental.pallas import tpu as pltpu
from jax.sharding import PartitionSpec as P

MESH = pl.DeviceIdType.MESH
HD = 128
SCALE = 1.0 / HD**0.5
LOG2E = math.log2(math.e)
BF = jnp.bfloat16
F32 = jnp.float32
NT = (((1,), (1,)), ((), ()))
NN = (((1,), (0,)), ((), ()))
Q, K, V, G, BIAS, DELTA = range(6)
STAT = 6


def each(count, body):
    lax.fori_loop(0, count, lambda i, c: (body(i), c)[1], 0)


def dot(a, b, dims):
    return lax.dot_general(a, b, dims, preferred_element_type=F32)


class Place:
    def __init__(self):
        self.c, self.t = lax.axis_index("ctx"), lax.axis_index("tp")
        self.z, self.yh = self.c // 2, self.c % 2
        self.yl, self.x, self.k = self.t // 8, (self.t % 8) // 2, self.t % 2
        self.y = self.yh * 2 + self.yl

    def other(self, d):
        return jnp.logical_or(d[0] != self.c, d[1] != self.t)

    def worker(self, u):
        return (self.t * 2 + self.yh, u)

    def home(self, s):
        return (s * 2 + self.yh, self.z)

    def group(self, u):
        return (self.c, u)

    def column(self, s):
        return (s * 2 + self.yh, self.t)

    def along_x(self, j):
        return (self.c, self.yl * 8 + ((self.x + j) % 4) * 2 + self.k)

    def along_y(self, j):
        y = (self.y + j) % 4
        return (self.z * 2 + y // 2, (y % 2) * 8 + self.x * 2 + self.k)

    def chip(self, j):
        return (self.c, ((self.t // 2) ^ j) * 2 + self.k)

    def sibling(self):
        return (self.c, self.t + 1 - 2 * self.k)


def kernel(
    q_ref, k_ref, v_ref, o_ref, og_ref, w_ref, tok_ref, out_ref,
    og, w, qi, ki, vi, oi, gi, brow, drow, dsend, relay, drelay,
    qg, kg, vg, gg, bg, dg, st, e, ms, kt, bt, xb,
    dv, dk, dqo, rss, rsr, fin, outs,
    word, ld, p0s, p0r, rls, rlr, a2s, a2r, ags, agr, rs_s, rs_r, ret_s, ret_r,
):
    me = Place()

    drains, pend = [], {}

    def finish():
        for wait in list(pend.values()) + drains:
            wait()
        out_ref[...] = outs[...]

    def remote(src, dst, s, r, d):
        return pltpu.make_async_remote_copy(src, dst, s, r, device_id=d, device_id_type=MESH)

    def landed(buf, sem):
        return lambda: pltpu.make_async_copy(buf, buf, sem).wait()

    barrier = pltpu.get_barrier_semaphore()

    def greet(d):
        pl.semaphore_signal(barrier, inc=1, device_id=d, device_id_type=MESH)

    each(15, lambda i: greet(me.group((me.t + i + 1) % 16)))
    for l in range(2):
        greet((me.z * 2 + 1 - me.yh, l * 8 + me.x * 2 + me.k))
    for j in (1, 15):
        greet(me.column((me.z + j) % 16))
    expected = 19
    apart = me.t != me.z

    def tell(step):
        for j in (2**step, 16 - 2**step):
            d = me.column((me.z + j) % 16)
            pl.semaphore_signal(word.at[step], inc=1, device_id=d, device_id_type=MESH)

    def told(step):
        pl.semaphore_wait(word.at[step], 2)

    def og_at(slot):
        return og.at[:, pl.ds(pl.multiple_of(slot * 384, 128), 384)]

    mine = og_at(me.t)
    loads = [
        pltpu.make_async_copy(src, dst, ld.at[i])
        for i, (src, dst) in enumerate(
            ((og_ref, mine), (q_ref, qi), (k_ref, ki), (v_ref, vi), (w_ref, w), (o_ref, oi))
        )
    ]
    for i, c in enumerate(loads):
        c.start()
        pend["load", i] = c.wait

    def loaded(i):
        pend.pop(("load", i))()

    brow[...] = jnp.log(tok_ref[...].astype(F32)).astype(BF).astype(F32)
    loaded(0)
    pl.semaphore_wait(barrier, expected)
    tell(0)

    def part(a):
        return lambda u: a.at[pl.ds(pl.multiple_of((u // 8 * 4 + u % 8 // 2) * 16, 16), 16), pl.ds(pl.multiple_of((u % 2) * 128, 128), 128)]

    here = pl.ds(pl.multiple_of(me.z * 16, 16), 16)
    routes = {
        Q: (part(qi), relay.at[0], qg.at[me.x, here], qg.at[me.x]),
        K: (part(ki), relay.at[1], kg.at[me.y, here], kg.at[me.y]),
        V: (part(vi), relay.at[2], vg.at[me.y, here], vg.at[me.y]),
        G: (part(gi), relay.at[3], gg.at[me.x, here], gg.at[me.x]),
        DELTA: (lambda u: dsend.at[u], drelay, dg.at[me.x, me.z], dg.at[me.x]),
        BIAS: (None, None, bg.at[me.y, me.z], bg.at[me.y]),
    }

    def spread(kind):
        src, mid, _, _ = routes[kind]
        pltpu.make_async_copy(src(me.t), mid.at[me.t], rlr.at[kind]).start()

        def one(i):
            u = (me.t + i + 1) % 16
            remote(src(u), mid.at[me.t], rls.at[kind], rlr.at[kind], me.group(u)).start()

        each(15, one)
        drains.append(landed(mid.at[0:15], rls.at[kind]))
        pend["relay", kind] = landed(mid, rlr.at[kind])

    def climb(kind):
        _, mid, dst, whole = routes[kind]
        src = (lambda s: brow) if mid is None else (lambda s: mid.at[s])
        if mid is not None:
            pend.pop(("relay", kind))()
        pltpu.make_async_copy(src(me.z), dst, a2r.at[kind]).start()

        def one(i):
            s = (me.z + 1 + (i + 7) % 15) % 16
            remote(src(s), dst, a2s.at[kind], a2r.at[kind], me.column(s)).start()

        each(15, one)
        sent = bg.at[0, 0:15] if mid is None else mid.at[0:15]
        drains.append(landed(sent, a2s.at[kind]))
        pend["a2a", kind] = landed(whole, a2r.at[kind])

    def arrived(kind):
        pend.pop(("a2a", kind))()

    loaded(1)
    spread(Q)
    told(0)
    tell(1)
    loaded(2)
    spread(K)

    def push(i):
        remote(mine, mine, p0s.at[0], p0r.at[me.t], me.chip(i + 1)).start()

    each(7, push)
    remote(mine, mine, p0s.at[0], p0r.at[me.t], me.sibling()).start()
    drains.append(landed(og.at[:, 0:3072], p0s.at[0]))
    sib = me.t + 1 - 2 * me.k
    pend["og", 0] = landed(og_at(sib), p0r.at[sib])

    def pushed(i):
        near = ((me.t // 2) ^ (i + 1)) * 2 + me.k
        landed(og_at(near), p0r.at[near])()

    pend["og", 1] = lambda: each(7, pushed)
    def share(kind, buf, own, along):
        def one(i):
            remote(buf.at[own], buf.at[own], ags.at[kind], agr.at[kind, own], along(i + 1)).start()

        def wait(i):
            n = (own + i + 1) % 4
            landed(buf.at[n], agr.at[kind, n])()

        each(3, one)
        drains.append(landed(buf.at[0:3], ags.at[kind]))
        pend["ag", kind] = lambda: each(3, wait)

    def shared(kind):
        pend.pop(("ag", kind))()

    loaded(4)
    for key in [key for key in pend if key[0] == "og"]:
        del pend[key]
    def features(chip):
        cols = pl.ds(pl.multiple_of(chip * 768, 128), 768)
        return dot(og[:, cols], w[:, cols], NT)

    def gather(i, acc):
        chip, last = (me.t // 2) ^ i, (me.t // 2) ^ (i - 1)
        near, far = chip * 2 + me.k, last * 2 + 1 - me.k
        block = og_at(near)
        landed(block, p0r.at[near])()
        remote(block, block, p0s.at[1], p0r.at[near], me.sibling()).start()
        landed(og_at(far), p0r.at[far])()
        return acc + features(last)

    told(1)
    tell(2)
    loaded(3)
    spread(V)
    told(2)
    climb(Q)
    climb(K)
    climb(BIAS)
    acc = lax.fori_loop(1, 8, gather, jnp.zeros((128, 256), F32))
    last = (me.t // 2) ^ 7
    landed(og_at(last * 2 + 1 - me.k), p0r.at[last * 2 + 1 - me.k])()
    acc = acc + features(last)
    drains.append(landed(og.at[:, 0:2688], p0s.at[1]))
    g = acc.astype(BF)
    gi[...] = g
    spread(G)
    climb(V)

    loaded(5)
    prod = g.astype(F32) * oi[...].astype(F32)
    lane = lax.broadcasted_iota(jnp.int32, (8, 128), 1)
    keep = (lane // 16) == me.z % 8
    for r in range(2):
        row = jnp.sum(jnp.transpose(prod[:, r * 128 : (r + 1) * 128]), axis=0, keepdims=True)
        drow[r] = jnp.broadcast_to(row, (8, 128))

    def lay(u):
        piece = u // 8 * 4 + u % 8 // 2
        rows = pltpu.roll(drow[u % 2], (me.z * 16 - piece * 16 + 256) % 128, 1)
        dsend[u] = jnp.where(keep, rows, 0.0)[0:1]

    each(16, lay)
    spread(DELTA)
    arrived(Q)
    share(Q, qg, me.x, me.along_x)
    arrived(K)
    share(K, kg, me.y, me.along_y)
    arrived(BIAS)
    share(BIAS, bg, me.y, me.along_y)
    climb(G)
    climb(DELTA)

    shared(BIAS)
    sub = lax.broadcasted_iota(jnp.int32, (16, 128), 0)
    lane = lax.broadcasted_iota(jnp.int32, (16, 128), 1)

    def bias_rows(i):
        hit = lane == ((i // 16 % 2) * 4 + me.x) * 16 + sub
        row = jnp.broadcast_to(bg[i // 16, i % 16], (16, 128))
        xb[pl.ds(pl.multiple_of(i * 16, 16), 16), :] = jnp.where(hit, row, 0.0).astype(BF)

    each(64, bias_rows)
    bt[...] = dot(xb[...], jnp.ones((128, 128), BF), NN) * LOG2E
    shared(K)
    shared(Q)

    def score(j, carry):
        x = (me.x + j) % 4
        keys = kg[...].reshape(1024, 128)
        bias = bt[...]
        s = dot(keys, qg[x], NT) * (SCALE * LOG2E) + jnp.concatenate([bias, bias], axis=1)
        m = jnp.max(s, axis=0, keepdims=True)
        p = jnp.exp2(s - m)
        e[x] = p
        ms[x] = m
        st[me.x, x] = m + jnp.log2(jnp.sum(p, axis=0, keepdims=True))
        return carry

    arrived(G)
    share(G, gg, me.x, me.along_x)
    lax.fori_loop(0, 4, score, 0)
    share(STAT, st, me.x, me.along_x)

    def turn(y):
        kt[:, pl.ds(pl.multiple_of(y * 256, 256), 256)] = jnp.transpose(kg[y].astype(F32)).astype(BF)


    arrived(DELTA)
    share(DELTA, dg, me.x, me.along_x)
    arrived(V)
    share(V, vg, me.y, me.along_y)
    each(4, turn)
    shared(STAT)

    dv[...] = jnp.zeros_like(dv)
    dk[...] = jnp.zeros_like(dk)

    def to_sum(i, own, n, d):
        return remote(rss.at[i, n], rsr.at[i, own], rs_s.at[i], rs_r.at[i, own], d)

    def summed(i, own):
        def wait(j):
            n = (own + j + 1) % 4
            landed(rsr.at[i, n], rs_r.at[i, n])()

        drains.append(landed(rss.at[i, 0:3], rs_s.at[i]))
        pend["rs", i] = lambda: each(3, wait)

    def push_sums(i, total):
        def one(j):
            y = (me.y + j + 1) % 4
            rows = total[pl.ds(pl.multiple_of(y * 256, 256), 256), :]
            rss[i, y] = (rows * SCALE if i == 1 else rows).astype(BF)
            to_sum(i, me.y, y, me.along_y(j + 1)).start()

        each(3, one)
        summed(i, me.y)

    pend.pop(("ag", G))

    def weigh(j, carry):
        x = (me.x + (j ^ (j // 2))) % 4
        pl.when(j > 0)(landed(gg.at[x], agr.at[G, x]))
        parts = [st[i, x] for i in range(4)]
        top = functools.reduce(jnp.maximum, parts)
        lse = top + jnp.log2(sum(jnp.exp2(a - top) for a in parts))
        p = e[x] * jnp.exp2(ms[x] - lse)
        e[x] = p
        dv[...] += dot(p.astype(BF), gg[x], NN)
        return carry

    lax.fori_loop(0, 4, weigh, 0)
    push_sums(2, dv)
    shared(DELTA)
    shared(V)

    def give(i):
        piece = me.yl * 4 + me.x
        dst = outs.at[
            i, pl.ds(pl.multiple_of(piece * 16, 16), 16), pl.ds(pl.multiple_of(me.k * 128, 128), 128)
        ]

        def src(s):
            return fin.at[i, pl.ds(pl.multiple_of(s * 16, 16), 16)]

        def one(j):
            s = (me.z + 1 + (j + 7) % 15) % 16
            remote(src(s), dst, ret_s.at[i, 0], ret_r.at[i], me.home(s)).start()

        each(15, one)
        last = remote(src(me.z), dst, ret_s.at[i, 1], ret_r.at[i], me.home(me.z))
        pl.when(apart)(lambda: last.start())
        pl.when(jnp.logical_not(apart))(lambda: pltpu.make_async_copy(src(me.z), dst, ret_r.at[i]).start())
        drains.append(landed(fin.at[i, 0:240], ret_s.at[i, 0]))
        drains.append(lambda: pl.when(apart)(lambda: last.wait_send()))
        pend["ret", i] = landed(outs.at[i], ret_r.at[i])

    def settle(i):
        own = me.x if i == 0 else me.y
        if i == 0:
            total = dqo[...]
        else:
            total = (dv if i == 2 else dk)[pl.ds(pl.multiple_of(me.y * 256, 256), 256), :]
            total = total * SCALE if i == 1 else total
        pend.pop(("rs", i))()
        for j in (1, 3, 2):
            total = total + rsr[i, (own + j) % 4].astype(F32)
        fin[i] = total.astype(BF)
        give(i)

    def grads(j, carry):
        x = (me.x + 1 + j) % 4
        delta = jnp.concatenate([jnp.sum(dg[x, 0:8], axis=0), jnp.sum(dg[x, 8:16], axis=0)], axis=1)
        dp = dot(vg[...].reshape(1024, 128), gg[x], NT)
        ds = (e[x] * (dp - delta)).astype(BF)
        dk[...] += dot(ds, qg[x], NN)
        dq = jnp.transpose(dot(kt[...], ds, NN)) * SCALE

        @pl.when(j == 3)
        def _():
            dqo[...] = dq

        @pl.when(j < 3)
        def _():
            rss[0, x] = dq.astype(BF)
            to_sum(0, me.x, x, (me.c, me.yl * 8 + x * 2 + me.k)).start()

        return carry

    lax.fori_loop(0, 4, grads, 0)
    summed(0, me.x)
    push_sums(1, dk)

    settle(2)
    settle(0)
    settle(1)
    finish()


def split(a_ref, q_ref, k_ref, v_ref, a, into, out):
    outs = (q_ref, k_ref, v_ref)
    first = [pltpu.make_async_copy(a_ref.at[i], a.at[i], into.at[i]) for i in range(3)]
    then = [pltpu.make_async_copy(a.at[i], outs[i], out.at[i]) for i in range(3)]
    for c in first:
        c.start()
    for c, d in zip(first, then):
        c.wait()
        d.start()
    for d in then:
        d.wait()


def local(queries, keys, values, attn_out, out_grad, out_weight, token_sizes):
    any_ = pl.BlockSpec(memory_space=pl.ANY)
    vmem = pl.BlockSpec(memory_space=pltpu.VMEM)
    dma = pltpu.SemaphoreType.DMA
    scratch = [
        pltpu.VMEM((128, 6144), BF),
        pltpu.VMEM((256, 6144), BF),
        pltpu.VMEM((128, 256), BF),
        pltpu.VMEM((128, 256), BF),
        pltpu.VMEM((128, 256), BF),
        pltpu.VMEM((128, 256), BF),
        pltpu.VMEM((128, 256), BF),
        pltpu.VMEM((1, 128), F32),
        pltpu.VMEM((2, 8, 128), F32),
        pltpu.VMEM((16, 1, 128), F32),
        pltpu.VMEM((4, 16, 16, 128), BF),
        pltpu.VMEM((16, 1, 128), F32),
        pltpu.VMEM((4, 256, 128), BF),
        pltpu.VMEM((4, 256, 128), BF),
        pltpu.VMEM((4, 256, 128), BF),
        pltpu.VMEM((4, 256, 128), BF),
        pltpu.VMEM((4, 16, 1, 128), F32),
        pltpu.VMEM((4, 16, 1, 128), F32),
        pltpu.VMEM((4, 4, 1, 256), F32),
        pltpu.VMEM((4, 1024, 256), F32),
        pltpu.VMEM((4, 1, 256), F32),
        pltpu.VMEM((128, 1024), BF),
        pltpu.VMEM((1024, 128), F32),
        pltpu.VMEM((1024, 128), BF),
        pltpu.VMEM((1024, 128), F32),
        pltpu.VMEM((1024, 128), F32),
        pltpu.VMEM((256, 128), F32),
        pltpu.VMEM((3, 4, 256, 128), BF),
        pltpu.VMEM((3, 4, 256, 128), BF),
        pltpu.VMEM((3, 256, 128), BF),
        pltpu.VMEM((3, 128, 256), BF),
        pltpu.SemaphoreType.REGULAR((3,)),
        dma((6,)),
        dma((2,)),
        dma((16,)),
        dma((6,)),
        dma((6,)),
        dma((6,)),
        dma((6,)),
        dma((7,)),
        dma((7, 4)),
        dma((3,)),
        dma((3, 4)),
        dma((3, 2)),
        dma((3,)),
    ]
    stacked = pl.pallas_call(
        kernel,
        out_shape=jax.ShapeDtypeStruct((3, 128, 256), BF),
        in_specs=[any_] * 6 + [vmem],
        out_specs=vmem,
        scratch_shapes=scratch,
        compiler_params=pltpu.CompilerParams(
            collective_id=0, has_side_effects=True, vmem_limit_bytes=62 * 2**20
        ),
        cost_estimate=pl.CostEstimate(flops=2 * 10**9, bytes_accessed=4 * 10**6, transcendentals=10**6),
        name="attention_backward",
    )(queries, keys, values, attn_out, out_grad, out_weight, token_sizes.reshape(1, 128))
    shape = jax.ShapeDtypeStruct((128, 256), BF)
    return pl.pallas_call(
        split,
        out_shape=(shape, shape, shape),
        in_specs=[any_],
        out_specs=(any_, any_, any_),
        scratch_shapes=[pltpu.VMEM((3, 128, 256), BF), dma((3,)), dma((3,))],
        compiler_params=pltpu.CompilerParams(vmem_limit_bytes=62 * 2**20),
        name="split_outputs",
    )(stacked)


def solution(mesh):
    rows = P("ctx", "tp")
    return jax.shard_map(
        local,
        mesh=mesh,
        in_specs=(rows, rows, rows, rows, rows, P("tp", None), P("ctx")),
        out_specs=(rows, rows, rows),
        check_vma=False,
    )
```

```python
import functools
import math

import jax
import jax.numpy as jnp
from jax import lax
from jax.experimental import pallas as pl
from jax.experimental.pallas import tpu as pltpu
from jax.sharding import PartitionSpec as P

MESH = pl.DeviceIdType.MESH
HD = 128
SCALE = 1.0 / HD**0.5
LOG2E = math.log2(math.e)
BF = jnp.bfloat16
F32 = jnp.float32
NT = (((1,), (1,)), ((), ()))
NN = (((1,), (0,)), ((), ()))
Q, K, V, G, BIAS, DELTA = range(6)
STAT = 6


def each(count, body):
    lax.fori_loop(0, count, lambda i, c: (body(i), c)[1], 0)


def dot(a, b, dims):
    return lax.dot_general(a, b, dims, preferred_element_type=F32)


class Place:
    def __init__(self):
        self.c, self.t = lax.axis_index("ctx"), lax.axis_index("tp")
        self.z, self.yh = self.c // 2, self.c % 2
        self.yl, self.x, self.k = self.t // 8, (self.t % 8) // 2, self.t % 2
        self.y = self.yh * 2 + self.yl

    def other(self, d):
        return jnp.logical_or(d[0] != self.c, d[1] != self.t)

    def worker(self, u):
        return (self.t * 2 + self.yh, u)

    def home(self, s):
        return (s * 2 + self.yh, self.z)

    def group(self, u):
        return (self.c, u)

    def column(self, s):
        return (s * 2 + self.yh, self.t)

    def along_x(self, j):
        return (self.c, self.yl * 8 + ((self.x + j) % 4) * 2 + self.k)

    def along_y(self, j):
        y = (self.y + j) % 4
        return (self.z * 2 + y // 2, (y % 2) * 8 + self.x * 2 + self.k)

    def chip(self, j):
        return (self.c, ((self.t // 2) ^ j) * 2 + self.k)

    def sibling(self):
        return (self.c, self.t + 1 - 2 * self.k)


def kernel(
    q_ref, k_ref, v_ref, o_ref, og_ref, w_ref, tok_ref, out_ref,
    tok, og, w, qi, ki, vi, oi, gi, brow, drow, dsend, relay, drelay,
    qg, kg, vg, gg, bg, dg, st, e, ms, kt, bt, xb,
    dv, dk, dqo, rss, rsr, fin, outs,
    word, ld, od, p0s, p0r, rls, rlr, a2s, a2r, ags, agr, rs_s, rs_r, ret_s, ret_r,
):
    me = Place()

    drains, pend = [], {}

    def finish():
        for wait in list(pend.values()) + drains:
            wait()

    def remote(src, dst, s, r, d):
        return pltpu.make_async_remote_copy(src, dst, s, r, device_id=d, device_id_type=MESH)

    def landed(buf, sem):
        return lambda: pltpu.make_async_copy(buf, buf, sem).wait()

    barrier = pltpu.get_barrier_semaphore()

    def greet(d):
        pl.semaphore_signal(barrier, inc=1, device_id=d, device_id_type=MESH)

    each(15, lambda i: greet(me.group((me.t + i + 1) % 16)))
    for l in range(2):
        greet((me.z * 2 + 1 - me.yh, l * 8 + me.x * 2 + me.k))
    for j in (1, 15):
        greet(me.column((me.z + j) % 16))
    expected = 19
    apart = me.t != me.z

    def tell(step):
        for j in (2**step, 16 - 2**step):
            d = me.column((me.z + j) % 16)
            pl.semaphore_signal(word.at[step], inc=1, device_id=d, device_id_type=MESH)

    def told(step):
        pl.semaphore_wait(word.at[step], 2)

    def og_at(slot):
        return og.at[:, pl.ds(pl.multiple_of(slot * 384, 128), 384)]

    mine = og_at(me.t)
    loads = [
        pltpu.make_async_copy(src, dst, ld.at[i])
        for i, (src, dst) in enumerate(
            ((og_ref, mine), (q_ref, qi), (k_ref, ki), (v_ref, vi), (w_ref, w), (o_ref, oi), (tok_ref, tok))
        )
    ]
    for i, c in enumerate(loads):
        c.start()
        pend["load", i] = c.wait

    def loaded(i):
        pend.pop(("load", i))()

    loaded(0)
    pl.semaphore_wait(barrier, expected)
    tell(0)

    def part(a):
        return lambda u: a.at[pl.ds(pl.multiple_of((u // 8 * 4 + u % 8 // 2) * 16, 16), 16), pl.ds(pl.multiple_of((u % 2) * 128, 128), 128)]

    here = pl.ds(pl.multiple_of(me.z * 16, 16), 16)
    routes = {
        Q: (part(qi), relay.at[0], qg.at[me.x, here], qg.at[me.x]),
        K: (part(ki), relay.at[1], kg.at[me.y, here], kg.at[me.y]),
        V: (part(vi), relay.at[2], vg.at[me.y, here], vg.at[me.y]),
        G: (part(gi), relay.at[3], gg.at[me.x, here], gg.at[me.x]),
        DELTA: (lambda u: dsend.at[u], drelay, dg.at[me.x, me.z], dg.at[me.x]),
        BIAS: (None, None, bg.at[me.y, me.z], bg.at[me.y]),
    }

    def spread(kind):
        src, mid, _, _ = routes[kind]
        pltpu.make_async_copy(src(me.t), mid.at[me.t], rlr.at[kind]).start()

        def one(i):
            u = (me.t + i + 1) % 16
            remote(src(u), mid.at[me.t], rls.at[kind], rlr.at[kind], me.group(u)).start()

        each(15, one)
        drains.append(landed(mid.at[0:15], rls.at[kind]))
        pend["relay", kind] = landed(mid, rlr.at[kind])

    def climb(kind):
        _, mid, dst, whole = routes[kind]
        src = (lambda s: brow) if mid is None else (lambda s: mid.at[s])
        if mid is not None:
            pend.pop(("relay", kind))()
        pltpu.make_async_copy(src(me.z), dst, a2r.at[kind]).start()

        def one(i):
            s = (me.z + 1 + (i + 7) % 15) % 16
            remote(src(s), dst, a2s.at[kind], a2r.at[kind], me.column(s)).start()

        each(15, one)
        sent = bg.at[0, 0:15] if mid is None else mid.at[0:15]
        drains.append(landed(sent, a2s.at[kind]))
        pend["a2a", kind] = landed(whole, a2r.at[kind])

    def arrived(kind):
        pend.pop(("a2a", kind))()

    loaded(1)
    spread(Q)
    told(0)
    tell(1)
    loaded(2)
    spread(K)

    def push(i):
        remote(mine, mine, p0s.at[0], p0r.at[me.t], me.chip(i + 1)).start()

    each(7, push)
    remote(mine, mine, p0s.at[0], p0r.at[me.t], me.sibling()).start()
    drains.append(landed(og.at[:, 0:3072], p0s.at[0]))
    sib = me.t + 1 - 2 * me.k
    pend["og", 0] = landed(og_at(sib), p0r.at[sib])

    def pushed(i):
        near = ((me.t // 2) ^ (i + 1)) * 2 + me.k
        landed(og_at(near), p0r.at[near])()

    pend["og", 1] = lambda: each(7, pushed)
    def share(kind, buf, own, along):
        def one(i):
            remote(buf.at[own], buf.at[own], ags.at[kind], agr.at[kind, own], along(i + 1)).start()

        def wait(i):
            n = (own + i + 1) % 4
            landed(buf.at[n], agr.at[kind, n])()

        each(3, one)
        drains.append(landed(buf.at[0:3], ags.at[kind]))
        pend["ag", kind] = lambda: each(3, wait)

    def shared(kind):
        pend.pop(("ag", kind))()

    loaded(4)
    for key in [key for key in pend if key[0] == "og"]:
        del pend[key]
    def features(chip):
        cols = pl.ds(pl.multiple_of(chip * 768, 128), 768)
        return dot(og[:, cols], w[:, cols], NT)

    def gather(i, acc):
        chip, last = (me.t // 2) ^ i, (me.t // 2) ^ (i - 1)
        near, far = chip * 2 + me.k, last * 2 + 1 - me.k
        block = og_at(near)
        landed(block, p0r.at[near])()
        remote(block, block, p0s.at[1], p0r.at[near], me.sibling()).start()
        landed(og_at(far), p0r.at[far])()
        return acc + features(last)

    told(1)
    tell(2)
    loaded(3)
    spread(V)
    told(2)
    climb(Q)
    climb(K)
    loaded(6)
    brow[...] = jnp.log(tok[...].astype(F32)).astype(BF).astype(F32)
    climb(BIAS)
    acc = lax.fori_loop(1, 8, gather, jnp.zeros((128, 256), F32))
    last = (me.t // 2) ^ 7
    landed(og_at(last * 2 + 1 - me.k), p0r.at[last * 2 + 1 - me.k])()
    acc = acc + features(last)
    drains.append(landed(og.at[:, 0:2688], p0s.at[1]))
    g = acc.astype(BF)
    gi[...] = g
    spread(G)
    climb(V)

    loaded(5)
    prod = g.astype(F32) * oi[...].astype(F32)
    lane = lax.broadcasted_iota(jnp.int32, (8, 128), 1)
    keep = (lane // 16) == me.z % 8
    for r in range(2):
        row = jnp.sum(jnp.transpose(prod[:, r * 128 : (r + 1) * 128]), axis=0, keepdims=True)
        drow[r] = jnp.broadcast_to(row, (8, 128))

    def lay(u):
        piece = u // 8 * 4 + u % 8 // 2
        rows = pltpu.roll(drow[u % 2], (me.z * 16 - piece * 16 + 256) % 128, 1)
        dsend[u] = jnp.where(keep, rows, 0.0)[0:1]

    each(16, lay)
    spread(DELTA)
    arrived(Q)
    share(Q, qg, me.x, me.along_x)
    arrived(K)
    share(K, kg, me.y, me.along_y)
    arrived(BIAS)
    share(BIAS, bg, me.y, me.along_y)
    climb(G)
    climb(DELTA)

    shared(BIAS)
    sub = lax.broadcasted_iota(jnp.int32, (16, 128), 0)
    lane = lax.broadcasted_iota(jnp.int32, (16, 128), 1)

    def bias_rows(i):
        hit = lane == ((i // 16 % 2) * 4 + me.x) * 16 + sub
        row = jnp.broadcast_to(bg[i // 16, i % 16], (16, 128))
        xb[pl.ds(pl.multiple_of(i * 16, 16), 16), :] = jnp.where(hit, row, 0.0).astype(BF)

    each(64, bias_rows)
    bt[...] = dot(xb[...], jnp.ones((128, 128), BF), NN) * LOG2E
    shared(K)
    shared(Q)

    def score(j, carry):
        x = (me.x + j) % 4
        keys = kg[...].reshape(1024, 128)
        bias = bt[...]
        s = dot(keys, qg[x], NT) * (SCALE * LOG2E) + jnp.concatenate([bias, bias], axis=1)
        m = jnp.max(s, axis=0, keepdims=True)
        p = jnp.exp2(s - m)
        e[x] = p
        ms[x] = m
        st[me.x, x] = m + jnp.log2(jnp.sum(p, axis=0, keepdims=True))
        return carry

    arrived(G)
    share(G, gg, me.x, me.along_x)
    lax.fori_loop(0, 4, score, 0)
    share(STAT, st, me.x, me.along_x)

    def turn(y):
        kt[:, pl.ds(pl.multiple_of(y * 256, 256), 256)] = jnp.transpose(kg[y].astype(F32)).astype(BF)


    arrived(DELTA)
    share(DELTA, dg, me.x, me.along_x)
    arrived(V)
    share(V, vg, me.y, me.along_y)
    each(4, turn)
    shared(STAT)

    dv[...] = jnp.zeros_like(dv)
    dk[...] = jnp.zeros_like(dk)

    def to_sum(i, own, n, d):
        return remote(rss.at[i, n], rsr.at[i, own], rs_s.at[i], rs_r.at[i, own], d)

    def summed(i, own):
        def wait(j):
            n = (own + j + 1) % 4
            landed(rsr.at[i, n], rs_r.at[i, n])()

        drains.append(landed(rss.at[i, 0:3], rs_s.at[i]))
        pend["rs", i] = lambda: each(3, wait)

    def push_sums(i, total):
        def one(j):
            y = (me.y + j + 1) % 4
            rows = total[pl.ds(pl.multiple_of(y * 256, 256), 256), :]
            rss[i, y] = (rows * SCALE if i == 1 else rows).astype(BF)
            to_sum(i, me.y, y, me.along_y(j + 1)).start()

        each(3, one)
        summed(i, me.y)

    pend.pop(("ag", G))

    def weigh(j, carry):
        x = (me.x + (j ^ (j // 2))) % 4
        pl.when(j > 0)(landed(gg.at[x], agr.at[G, x]))
        parts = [st[i, x] for i in range(4)]
        top = functools.reduce(jnp.maximum, parts)
        lse = top + jnp.log2(sum(jnp.exp2(a - top) for a in parts))
        p = e[x] * jnp.exp2(ms[x] - lse)
        e[x] = p
        dv[...] += dot(p.astype(BF), gg[x], NN)
        return carry

    lax.fori_loop(0, 4, weigh, 0)
    push_sums(2, dv)
    shared(DELTA)
    shared(V)

    def give(i):
        piece = me.yl * 4 + me.x
        dst = outs.at[
            i, pl.ds(pl.multiple_of(piece * 16, 16), 16), pl.ds(pl.multiple_of(me.k * 128, 128), 128)
        ]

        def src(s):
            return fin.at[i, pl.ds(pl.multiple_of(s * 16, 16), 16)]

        def one(j):
            s = (me.z + 1 + (j + 7) % 15) % 16
            remote(src(s), dst, ret_s.at[i, 0], ret_r.at[i], me.home(s)).start()

        each(15, one)
        last = remote(src(me.z), dst, ret_s.at[i, 1], ret_r.at[i], me.home(me.z))
        pl.when(apart)(lambda: last.start())
        pl.when(jnp.logical_not(apart))(lambda: pltpu.make_async_copy(src(me.z), dst, ret_r.at[i]).start())
        drains.append(landed(fin.at[i, 0:240], ret_s.at[i, 0]))
        drains.append(lambda: pl.when(apart)(lambda: last.wait_send()))
        pend["ret", i] = landed(outs.at[i], ret_r.at[i])

    def settle(i):
        own = me.x if i == 0 else me.y
        if i == 0:
            total = dqo[...]
        else:
            total = (dv if i == 2 else dk)[pl.ds(pl.multiple_of(me.y * 256, 256), 256), :]
            total = total * SCALE if i == 1 else total
        pend.pop(("rs", i))()
        for j in (1, 3, 2):
            total = total + rsr[i, (own + j) % 4].astype(F32)
        fin[i] = total.astype(BF)
        give(i)

    def grads(j, carry):
        x = (me.x + 1 + j) % 4
        delta = jnp.concatenate([jnp.sum(dg[x, 0:8], axis=0), jnp.sum(dg[x, 8:16], axis=0)], axis=1)
        dp = dot(vg[...].reshape(1024, 128), gg[x], NT)
        ds = (e[x] * (dp - delta)).astype(BF)
        dk[...] += dot(ds, qg[x], NN)
        dq = jnp.transpose(dot(kt[...], ds, NN)) * SCALE

        @pl.when(j == 3)
        def _():
            dqo[...] = dq

        @pl.when(j < 3)
        def _():
            rss[0, x] = dq.astype(BF)
            to_sum(0, me.x, x, (me.c, me.yl * 8 + x * 2 + me.k)).start()

        return carry

    lax.fori_loop(0, 4, grads, 0)
    summed(0, me.x)
    push_sums(1, dk)

    settle(2)
    settle(0)
    settle(1)
    for i in (2, 0, 1):
        pend.pop(("ret", i))()
        c = pltpu.make_async_copy(outs.at[i], out_ref.at[i], od.at[i])
        c.start()
        drains.append(c.wait)
    finish()


def split(a_ref, q_ref, k_ref, v_ref, a, into, out):
    outs = (q_ref, k_ref, v_ref)
    first = [pltpu.make_async_copy(a_ref.at[i], a.at[i], into.at[i]) for i in range(3)]
    then = [pltpu.make_async_copy(a.at[i], outs[i], out.at[i]) for i in range(3)]
    for c in first:
        c.start()
    for c, d in zip(first, then):
        c.wait()
        d.start()
    for d in then:
        d.wait()


def local(queries, keys, values, attn_out, out_grad, out_weight, token_sizes):
    any_ = pl.BlockSpec(memory_space=pl.ANY)
    dma = pltpu.SemaphoreType.DMA
    scratch = [
        pltpu.VMEM((1, 128), jnp.int32),
        pltpu.VMEM((128, 6144), BF),
        pltpu.VMEM((256, 6144), BF),
        pltpu.VMEM((128, 256), BF),
        pltpu.VMEM((128, 256), BF),
        pltpu.VMEM((128, 256), BF),
        pltpu.VMEM((128, 256), BF),
        pltpu.VMEM((128, 256), BF),
        pltpu.VMEM((1, 128), F32),
        pltpu.VMEM((2, 8, 128), F32),
        pltpu.VMEM((16, 1, 128), F32),
        pltpu.VMEM((4, 16, 16, 128), BF),
        pltpu.VMEM((16, 1, 128), F32),
        pltpu.VMEM((4, 256, 128), BF),
        pltpu.VMEM((4, 256, 128), BF),
        pltpu.VMEM((4, 256, 128), BF),
        pltpu.VMEM((4, 256, 128), BF),
        pltpu.VMEM((4, 16, 1, 128), F32),
        pltpu.VMEM((4, 16, 1, 128), F32),
        pltpu.VMEM((4, 4, 1, 256), F32),
        pltpu.VMEM((4, 1024, 256), F32),
        pltpu.VMEM((4, 1, 256), F32),
        pltpu.VMEM((128, 1024), BF),
        pltpu.VMEM((1024, 128), F32),
        pltpu.VMEM((1024, 128), BF),
        pltpu.VMEM((1024, 128), F32),
        pltpu.VMEM((1024, 128), F32),
        pltpu.VMEM((256, 128), F32),
        pltpu.VMEM((3, 4, 256, 128), BF),
        pltpu.VMEM((3, 4, 256, 128), BF),
        pltpu.VMEM((3, 256, 128), BF),
        pltpu.VMEM((3, 128, 256), BF),
        pltpu.SemaphoreType.REGULAR((3,)),
        dma((7,)),
        dma((3,)),
        dma((2,)),
        dma((16,)),
        dma((6,)),
        dma((6,)),
        dma((6,)),
        dma((6,)),
        dma((7,)),
        dma((7, 4)),
        dma((3,)),
        dma((3, 4)),
        dma((3, 2)),
        dma((3,)),
    ]
    stacked = pl.pallas_call(
        kernel,
        out_shape=jax.ShapeDtypeStruct((3, 128, 256), BF),
        in_specs=[any_] * 7,
        out_specs=any_,
        scratch_shapes=scratch,
        compiler_params=pltpu.CompilerParams(
            collective_id=0, has_side_effects=True, vmem_limit_bytes=62 * 2**20
        ),
        cost_estimate=pl.CostEstimate(flops=2 * 10**9, bytes_accessed=4 * 10**6, transcendentals=10**6),
        name="attention_backward",
    )(queries, keys, values, attn_out, out_grad, out_weight, token_sizes.reshape(1, 128))
    shape = jax.ShapeDtypeStruct((128, 256), BF)
    return pl.pallas_call(
        split,
        out_shape=(shape, shape, shape),
        in_specs=[any_],
        out_specs=(any_, any_, any_),
        scratch_shapes=[pltpu.VMEM((3, 128, 256), BF), dma((3,)), dma((3,))],
        compiler_params=pltpu.CompilerParams(vmem_limit_bytes=62 * 2**20),
        name="split_outputs",
    )(stacked)


def solution(mesh):
    rows = P("ctx", "tp")
    return jax.shard_map(
        local,
        mesh=mesh,
        in_specs=(rows, rows, rows, rows, rows, P("tp", None), P("ctx")),
        out_specs=(rows, rows, rows),
        check_vma=False,
    )
```

```python
import functools
import math

import jax
import jax.numpy as jnp
from jax import lax
from jax.experimental import pallas as pl
from jax.experimental.pallas import tpu as pltpu
from jax.sharding import PartitionSpec as P

MESH = pl.DeviceIdType.MESH
HD = 128
SCALE = 1.0 / HD**0.5
LOG2E = math.log2(math.e)
BF = jnp.bfloat16
F32 = jnp.float32
NT = (((1,), (1,)), ((), ()))
NN = (((1,), (0,)), ((), ()))
Q, K, V, G, BIAS, DELTA = range(6)
STAT = 6


def each(count, body):
    lax.fori_loop(0, count, lambda i, c: (body(i), c)[1], 0)


def dot(a, b, dims):
    return lax.dot_general(a, b, dims, preferred_element_type=F32)


class Place:
    def __init__(self):
        self.c, self.t = lax.axis_index("ctx"), lax.axis_index("tp")
        self.z, self.yh = self.c // 2, self.c % 2
        self.yl, self.x, self.k = self.t // 8, (self.t % 8) // 2, self.t % 2
        self.y = self.yh * 2 + self.yl

    def other(self, d):
        return jnp.logical_or(d[0] != self.c, d[1] != self.t)

    def worker(self, u):
        return (self.t * 2 + self.yh, u)

    def home(self, s):
        return (s * 2 + self.yh, self.z)

    def group(self, u):
        return (self.c, u)

    def column(self, s):
        return (s * 2 + self.yh, self.t)

    def along_x(self, j):
        return (self.c, self.yl * 8 + ((self.x + j) % 4) * 2 + self.k)

    def along_y(self, j):
        y = (self.y + j) % 4
        return (self.z * 2 + y // 2, (y % 2) * 8 + self.x * 2 + self.k)

    def chip(self, j):
        return (self.c, ((self.t // 2) ^ j) * 2 + self.k)

    def sibling(self):
        return (self.c, self.t + 1 - 2 * self.k)


def kernel(
    q_ref, k_ref, v_ref, o_ref, og_ref, w_ref, tok_ref, out_ref,
    tok, og, w, qi, ki, vi, oi, gi, brow, drow, dsend, relay, drelay,
    qg, kg, vg, gg, bg, dg, st, e, ms, kt, bt, xb,
    dv, dk, dqo, rss, rsr, fin, outs,
    word, ld, od, p0s, p0r, rls, rlr, a2s, a2r, ags, agr, rs_s, rs_r, ret_s, ret_r,
):
    me = Place()

    drains, pend = [], {}

    def finish():
        for wait in list(pend.values()) + drains:
            wait()

    def remote(src, dst, s, r, d):
        return pltpu.make_async_remote_copy(src, dst, s, r, device_id=d, device_id_type=MESH)

    def landed(buf, sem):
        return lambda: pltpu.make_async_copy(buf, buf, sem).wait()

    barrier = pltpu.get_barrier_semaphore()

    def greet(d):
        pl.semaphore_signal(barrier, inc=1, device_id=d, device_id_type=MESH)

    for l in range(2):
        greet((me.z * 2 + 1 - me.yh, l * 8 + me.x * 2 + me.k))
    for j in (1, 15):
        greet(me.column((me.z + j) % 16))
    each(15, lambda i: greet(me.group((me.t + i + 1) % 16)))
    expected = 19
    apart = me.t != me.z

    def tell(step):
        for j in (2**step, 16 - 2**step):
            d = me.column((me.z + j) % 16)
            pl.semaphore_signal(word.at[step], inc=1, device_id=d, device_id_type=MESH)

    def told(step):
        pl.semaphore_wait(word.at[step], 2)

    def og_at(slot):
        return og.at[:, pl.ds(pl.multiple_of(slot * 384, 128), 384)]

    mine = og_at(me.t)
    loads = [
        pltpu.make_async_copy(src, dst, ld.at[i])
        for i, (src, dst) in enumerate(
            ((og_ref, mine), (q_ref, qi), (k_ref, ki), (v_ref, vi), (w_ref, w), (o_ref, oi), (tok_ref, tok))
        )
    ]
    for i, c in enumerate(loads):
        c.start()
        pend["load", i] = c.wait

    def loaded(i):
        pend.pop(("load", i))()

    loaded(0)
    pl.semaphore_wait(barrier, expected)
    tell(0)

    def part(a):
        return lambda u: a.at[pl.ds(pl.multiple_of((u // 8 * 4 + u % 8 // 2) * 16, 16), 16), pl.ds(pl.multiple_of((u % 2) * 128, 128), 128)]

    here = pl.ds(pl.multiple_of(me.z * 16, 16), 16)
    routes = {
        Q: (part(qi), relay.at[0], qg.at[me.x, here], qg.at[me.x]),
        K: (part(ki), relay.at[1], kg.at[me.y, here], kg.at[me.y]),
        V: (part(vi), relay.at[2], vg.at[me.y, here], vg.at[me.y]),
        G: (part(gi), relay.at[3], gg.at[me.x, here], gg.at[me.x]),
        DELTA: (lambda u: dsend.at[u], drelay, dg.at[me.x, me.z], dg.at[me.x]),
        BIAS: (None, None, bg.at[me.y, me.z], bg.at[me.y]),
    }

    def spread(kind):
        src, mid, _, _ = routes[kind]
        pltpu.make_async_copy(src(me.t), mid.at[me.t], rlr.at[kind]).start()

        def one(i):
            u = (me.t + i + 1) % 16
            remote(src(u), mid.at[me.t], rls.at[kind], rlr.at[kind], me.group(u)).start()

        each(15, one)
        drains.append(landed(mid.at[0:15], rls.at[kind]))
        pend["relay", kind] = landed(mid, rlr.at[kind])

    def climb(kind):
        _, mid, dst, whole = routes[kind]
        src = (lambda s: brow) if mid is None else (lambda s: mid.at[s])
        if mid is not None:
            pend.pop(("relay", kind))()
        pltpu.make_async_copy(src(me.z), dst, a2r.at[kind]).start()

        def one(i):
            s = (me.z + 1 + (i + 7) % 15) % 16
            remote(src(s), dst, a2s.at[kind], a2r.at[kind], me.column(s)).start()

        each(15, one)
        sent = bg.at[0, 0:15] if mid is None else mid.at[0:15]
        drains.append(landed(sent, a2s.at[kind]))
        pend["a2a", kind] = landed(whole, a2r.at[kind])

    def arrived(kind):
        pend.pop(("a2a", kind))()

    loaded(1)
    spread(Q)
    told(0)
    tell(1)
    loaded(2)
    spread(K)

    def push(i):
        remote(mine, mine, p0s.at[0], p0r.at[me.t], me.chip(i + 1)).start()

    each(7, push)
    remote(mine, mine, p0s.at[0], p0r.at[me.t], me.sibling()).start()
    drains.append(landed(og.at[:, 0:3072], p0s.at[0]))
    sib = me.t + 1 - 2 * me.k
    pend["og", 0] = landed(og_at(sib), p0r.at[sib])

    def pushed(i):
        near = ((me.t // 2) ^ (i + 1)) * 2 + me.k
        landed(og_at(near), p0r.at[near])()

    pend["og", 1] = lambda: each(7, pushed)
    def share(kind, buf, own, along):
        def one(i):
            remote(buf.at[own], buf.at[own], ags.at[kind], agr.at[kind, own], along(i + 1)).start()

        def wait(i):
            n = (own + i + 1) % 4
            landed(buf.at[n], agr.at[kind, n])()

        each(3, one)
        drains.append(landed(buf.at[0:3], ags.at[kind]))
        pend["ag", kind] = lambda: each(3, wait)

    def shared(kind):
        pend.pop(("ag", kind))()

    loaded(4)
    for key in [key for key in pend if key[0] == "og"]:
        del pend[key]
    def features(chip):
        cols = pl.ds(pl.multiple_of(chip * 768, 128), 768)
        return dot(og[:, cols], w[:, cols], NT)

    def gather(i, acc):
        chip, last = (me.t // 2) ^ i, (me.t // 2) ^ (i - 1)
        near, far = chip * 2 + me.k, last * 2 + 1 - me.k
        block = og_at(near)
        landed(block, p0r.at[near])()
        remote(block, block, p0s.at[1], p0r.at[near], me.sibling()).start()
        landed(og_at(far), p0r.at[far])()
        return acc + features(last)

    told(1)
    tell(2)
    loaded(3)
    spread(V)
    told(2)
    climb(Q)
    climb(K)
    loaded(6)
    brow[...] = jnp.log(tok[...].astype(F32)).astype(BF).astype(F32)
    climb(BIAS)
    acc = lax.fori_loop(1, 8, gather, jnp.zeros((128, 256), F32))
    last = (me.t // 2) ^ 7
    landed(og_at(last * 2 + 1 - me.k), p0r.at[last * 2 + 1 - me.k])()
    acc = acc + features(last)
    drains.append(landed(og.at[:, 0:2688], p0s.at[1]))
    g = acc.astype(BF)
    gi[...] = g
    spread(G)
    climb(V)

    loaded(5)
    prod = g.astype(F32) * oi[...].astype(F32)
    lane = lax.broadcasted_iota(jnp.int32, (8, 128), 1)
    keep = (lane // 16) == me.z % 8
    for r in range(2):
        row = jnp.sum(jnp.transpose(prod[:, r * 128 : (r + 1) * 128]), axis=0, keepdims=True)
        drow[r] = jnp.broadcast_to(row, (8, 128))

    def lay(u):
        piece = u // 8 * 4 + u % 8 // 2
        rows = pltpu.roll(drow[u % 2], (me.z * 16 - piece * 16 + 256) % 128, 1)
        dsend[u] = jnp.where(keep, rows, 0.0)[0:1]

    each(16, lay)
    spread(DELTA)
    arrived(Q)
    share(Q, qg, me.x, me.along_x)
    arrived(K)
    share(K, kg, me.y, me.along_y)
    arrived(BIAS)
    share(BIAS, bg, me.y, me.along_y)
    climb(G)
    climb(DELTA)

    shared(BIAS)
    sub = lax.broadcasted_iota(jnp.int32, (16, 128), 0)
    lane = lax.broadcasted_iota(jnp.int32, (16, 128), 1)

    def bias_rows(i):
        hit = lane == ((i // 16 % 2) * 4 + me.x) * 16 + sub
        row = jnp.broadcast_to(bg[i // 16, i % 16], (16, 128))
        xb[pl.ds(pl.multiple_of(i * 16, 16), 16), :] = jnp.where(hit, row, 0.0).astype(BF)

    each(64, bias_rows)
    bt[...] = dot(xb[...], jnp.ones((128, 128), BF), NN) * LOG2E
    shared(K)
    shared(Q)

    def score(j, carry):
        x = (me.x + j) % 4
        keys = kg[...].reshape(1024, 128)
        bias = bt[...]
        s = dot(keys, qg[x], NT) * (SCALE * LOG2E) + jnp.concatenate([bias, bias], axis=1)
        m = jnp.max(s, axis=0, keepdims=True)
        p = jnp.exp2(s - m)
        e[x] = p
        ms[x] = m
        st[me.x, x] = m + jnp.log2(jnp.sum(p, axis=0, keepdims=True))
        return carry

    arrived(G)
    share(G, gg, me.x, me.along_x)
    lax.fori_loop(0, 4, score, 0)
    share(STAT, st, me.x, me.along_x)

    def turn(y):
        kt[:, pl.ds(pl.multiple_of(y * 256, 256), 256)] = jnp.transpose(kg[y].astype(F32)).astype(BF)


    arrived(DELTA)
    share(DELTA, dg, me.x, me.along_x)
    arrived(V)
    share(V, vg, me.y, me.along_y)
    each(4, turn)
    shared(STAT)

    dv[...] = jnp.zeros_like(dv)
    dk[...] = jnp.zeros_like(dk)

    def to_sum(i, own, n, d):
        return remote(rss.at[i, n], rsr.at[i, own], rs_s.at[i], rs_r.at[i, own], d)

    def summed(i, own):
        def wait(j):
            n = (own + j + 1) % 4
            landed(rsr.at[i, n], rs_r.at[i, n])()

        drains.append(landed(rss.at[i, 0:3], rs_s.at[i]))
        pend["rs", i] = lambda: each(3, wait)

    def push_sums(i, total):
        def one(j):
            y = (me.y + j + 1) % 4
            rows = total[pl.ds(pl.multiple_of(y * 256, 256), 256), :]
            rss[i, y] = (rows * SCALE if i == 1 else rows).astype(BF)
            to_sum(i, me.y, y, me.along_y(j + 1)).start()

        each(3, one)
        summed(i, me.y)

    pend.pop(("ag", G))

    def weigh(j, carry):
        x = (me.x + (j ^ (j // 2))) % 4
        pl.when(j > 0)(landed(gg.at[x], agr.at[G, x]))
        parts = [st[i, x] for i in range(4)]
        top = functools.reduce(jnp.maximum, parts)
        lse = top + jnp.log2(sum(jnp.exp2(a - top) for a in parts))
        p = e[x] * jnp.exp2(ms[x] - lse)
        e[x] = p
        dv[...] += dot(p.astype(BF), gg[x], NN)
        return carry

    lax.fori_loop(0, 4, weigh, 0)
    push_sums(2, dv)
    shared(DELTA)
    shared(V)

    def give(i):
        piece = me.yl * 4 + me.x
        dst = outs.at[
            i, pl.ds(pl.multiple_of(piece * 16, 16), 16), pl.ds(pl.multiple_of(me.k * 128, 128), 128)
        ]

        def src(s):
            return fin.at[i, pl.ds(pl.multiple_of(s * 16, 16), 16)]

        def one(j):
            s = (me.z + 1 + (j + 7) % 15) % 16
            remote(src(s), dst, ret_s.at[i, 0], ret_r.at[i], me.home(s)).start()

        each(15, one)
        last = remote(src(me.z), dst, ret_s.at[i, 1], ret_r.at[i], me.home(me.z))
        pl.when(apart)(lambda: last.start())
        pl.when(jnp.logical_not(apart))(lambda: pltpu.make_async_copy(src(me.z), dst, ret_r.at[i]).start())
        drains.append(landed(fin.at[i, 0:240], ret_s.at[i, 0]))
        drains.append(lambda: pl.when(apart)(lambda: last.wait_send()))
        pend["ret", i] = landed(outs.at[i], ret_r.at[i])

    def settle(i):
        own = me.x if i == 0 else me.y
        if i == 0:
            total = dqo[...]
        else:
            total = (dv if i == 2 else dk)[pl.ds(pl.multiple_of(me.y * 256, 256), 256), :]
            total = total * SCALE if i == 1 else total
        pend.pop(("rs", i))()
        for j in (1, 3, 2):
            total = total + rsr[i, (own + j) % 4].astype(F32)
        fin[i] = total.astype(BF)
        give(i)

    def grads(j, carry):
        x = (me.x + 1 + j) % 4
        delta = jnp.concatenate([jnp.sum(dg[x, 0:8], axis=0), jnp.sum(dg[x, 8:16], axis=0)], axis=1)
        dp = dot(vg[...].reshape(1024, 128), gg[x], NT)
        ds = (e[x] * (dp - delta)).astype(BF)
        dk[...] += dot(ds, qg[x], NN)
        dq = jnp.transpose(dot(kt[...], ds, NN)) * SCALE

        @pl.when(j == 3)
        def _():
            dqo[...] = dq

        @pl.when(j < 3)
        def _():
            rss[0, x] = dq.astype(BF)
            to_sum(0, me.x, x, (me.c, me.yl * 8 + x * 2 + me.k)).start()

        return carry

    lax.fori_loop(0, 4, grads, 0)
    summed(0, me.x)
    push_sums(1, dk)

    settle(2)
    settle(0)
    settle(1)
    for i in (2, 0, 1):
        pend.pop(("ret", i))()
        c = pltpu.make_async_copy(outs.at[i], out_ref.at[i], od.at[i])
        c.start()
        drains.append(c.wait)
    finish()


def split(a_ref, q_ref, k_ref, v_ref, a, into, out):
    outs = (q_ref, k_ref, v_ref)
    first = [pltpu.make_async_copy(a_ref.at[i], a.at[i], into.at[i]) for i in range(3)]
    then = [pltpu.make_async_copy(a.at[i], outs[i], out.at[i]) for i in range(3)]
    for c in first:
        c.start()
    for c, d in zip(first, then):
        c.wait()
        d.start()
    for d in then:
        d.wait()


def local(queries, keys, values, attn_out, out_grad, out_weight, token_sizes):
    any_ = pl.BlockSpec(memory_space=pl.ANY)
    dma = pltpu.SemaphoreType.DMA
    scratch = [
        pltpu.VMEM((1, 128), jnp.int32),
        pltpu.VMEM((128, 6144), BF),
        pltpu.VMEM((256, 6144), BF),
        pltpu.VMEM((128, 256), BF),
        pltpu.VMEM((128, 256), BF),
        pltpu.VMEM((128, 256), BF),
        pltpu.VMEM((128, 256), BF),
        pltpu.VMEM((128, 256), BF),
        pltpu.VMEM((1, 128), F32),
        pltpu.VMEM((2, 8, 128), F32),
        pltpu.VMEM((16, 1, 128), F32),
        pltpu.VMEM((4, 16, 16, 128), BF),
        pltpu.VMEM((16, 1, 128), F32),
        pltpu.VMEM((4, 256, 128), BF),
        pltpu.VMEM((4, 256, 128), BF),
        pltpu.VMEM((4, 256, 128), BF),
        pltpu.VMEM((4, 256, 128), BF),
        pltpu.VMEM((4, 16, 1, 128), F32),
        pltpu.VMEM((4, 16, 1, 128), F32),
        pltpu.VMEM((4, 4, 1, 256), F32),
        pltpu.VMEM((4, 1024, 256), F32),
        pltpu.VMEM((4, 1, 256), F32),
        pltpu.VMEM((128, 1024), BF),
        pltpu.VMEM((1024, 128), F32),
        pltpu.VMEM((1024, 128), BF),
        pltpu.VMEM((1024, 128), F32),
        pltpu.VMEM((1024, 128), F32),
        pltpu.VMEM((256, 128), F32),
        pltpu.VMEM((3, 4, 256, 128), BF),
        pltpu.VMEM((3, 4, 256, 128), BF),
        pltpu.VMEM((3, 256, 128), BF),
        pltpu.VMEM((3, 128, 256), BF),
        pltpu.SemaphoreType.REGULAR((3,)),
        dma((7,)),
        dma((3,)),
        dma((2,)),
        dma((16,)),
        dma((6,)),
        dma((6,)),
        dma((6,)),
        dma((6,)),
        dma((7,)),
        dma((7, 4)),
        dma((3,)),
        dma((3, 4)),
        dma((3, 2)),
        dma((3,)),
    ]
    stacked = pl.pallas_call(
        kernel,
        out_shape=jax.ShapeDtypeStruct((3, 128, 256), BF),
        in_specs=[any_] * 7,
        out_specs=any_,
        scratch_shapes=scratch,
        compiler_params=pltpu.CompilerParams(
            collective_id=0, has_side_effects=True, vmem_limit_bytes=62 * 2**20
        ),
        cost_estimate=pl.CostEstimate(flops=2 * 10**9, bytes_accessed=4 * 10**6, transcendentals=10**6),
        name="attention_backward",
    )(queries, keys, values, attn_out, out_grad, out_weight, token_sizes.reshape(1, 128))
    shape = jax.ShapeDtypeStruct((128, 256), BF)
    return pl.pallas_call(
        split,
        out_shape=(shape, shape, shape),
        in_specs=[any_],
        out_specs=(any_, any_, any_),
        scratch_shapes=[pltpu.VMEM((3, 128, 256), BF), dma((3,)), dma((3,))],
        compiler_params=pltpu.CompilerParams(vmem_limit_bytes=62 * 2**20),
        name="split_outputs",
    )(stacked)


def solution(mesh):
    rows = P("ctx", "tp")
    return jax.shard_map(
        local,
        mesh=mesh,
        in_specs=(rows, rows, rows, rows, rows, P("tp", None), P("ctx")),
        out_specs=(rows, rows, rows),
        check_vma=False,
    )
```
